256 devices in a mesh: oi: 4 (over x), oj: 8 (over z_hi, core), vert: 8 (over z_lo, y).
Axes of the slice: x: 4, y: 4, z: 8 (z_hi: 4, z_lo: 2; z = z_hi * 2 + z_lo), core: 2. Of those that a mesh axis runs over, the one named last changes fastest.
Arguments:
- amplitudes: bfloat16 [32, 32, 8, 128, 128], P('oi', 'oj'), may hold values from -6 to 6
- chol: bfloat16 [64, 256, 4, 128], P(('oj', 'vert')), may hold values from -0.078125 to 0.078125
- occ_irrep: int32 [32], replicated, may hold values from 0 to 7
Outputs:
- residual: float32 [32, 32, 8, 4, 4], P('oi', 'oj', 'vert')
The draws below stay inside these ranges and needn't reach their ends.
Inputs may be any that keep to these rules, and one draw needn't show every extreme that they name: `occ_irrep`: D2h irrep labels, multiplied by bitwise exclusive or.
All inputs are finite; a program needn't handle non-finite values.
Results may differ from the reference program's by a relative error of at most 0.0028.
Values may be sent and summed in bfloat16 or wider, within the bound.
No kernel may reach another device: no remote copies, remote signals or barrier semaphores. Data moves between devices by JAX's collectives and lax.ppermute only.
A program may use at most 192 MiB of HBM per device.

```python
import jax
import jax.numpy as jnp
from jax import lax

IRREPS = 8
VB = 128
PB = 256
WB = 4
NOCC = 32


def plant(values, rng, smallest, high):
    dims = values.shape
    place = [jax.random.randint(jax.random.fold_in(rng, axis), (), 0, dims[axis]) for axis in range(len(dims))]
    values = values.at[tuple(place)].set(smallest)
    longest = dims.index(max(dims))
    place[longest] = (place[longest] + 1) % dims[longest]
    return values.at[tuple(place)].set(high)


def steps_of(key, extent, split, smallest, largest):
    gain = 1.0
    for axis_at, parts in split:
        draws = jax.random.uniform(jax.random.fold_in(jax.random.fold_in(key, 6), axis_at), (parts,), jnp.float32, smallest / len(split), largest / len(split))
        gain = gain * jnp.repeat(jnp.exp(draws), extent[axis_at] // parts).reshape((-1,) + (1,) * (len(extent) - 1 - axis_at))
    return gain


def bell_draw(stream_key, dims, width, most, split=(), kind=jnp.bfloat16):
    values = width * jax.random.normal(stream_key, dims, jnp.float32)
    if split:
        values = values * steps_of(stream_key, dims, split, -0.22, 0.18)
    return jnp.clip(values, -most, most).astype(kind)


def setup_inputs(seed: int = 0) -> dict:
    key_of = jax.random.split(jax.random.key(seed), 4)
    amplitudes = bell_draw(key_of[0], (NOCC, NOCC, IRREPS, VB, VB), 1.0, 6.0, ((0, 4), (1, 8)))
    chol = bell_draw(key_of[1], (IRREPS * IRREPS, PB, WB, VB), (VB * (8 * PB) ** 0.5) ** -0.5, 0.078125, ((0, 64),))
    occ_irrep = plant(jax.random.randint(key_of[2], (NOCC,), 0, IRREPS), jax.random.fold_in(key_of[2], 1), 0, IRREPS - 1).astype(jnp.int32)
    return dict(amplitudes=amplitudes, chol=chol, occ_irrep=occ_irrep)


def reference(amplitudes, chol, occ_irrep):
    irreps = jnp.arange(IRREPS, dtype=jnp.int32)
    blocks = chol.reshape(IRREPS, IRREPS, PB, WB, VB)
    pair_irrep = jnp.bitwise_xor(occ_irrep[:, None], occ_irrep[None, :]).astype(jnp.int32)

    def one_pair(inputs):
        tile, sym = inputs

        def per_aux(totals, aux_irrep):
            chol_aux = blocks[aux_irrep].astype(jnp.float32)
            amp_blocks = tile[jnp.bitwise_xor(irreps, aux_irrep)].astype(jnp.float32)
            half_step = jnp.einsum('gpac,gcd->gpad', chol_aux, amp_blocks).astype(jnp.bfloat16)
            chol_sel = chol_aux[jnp.bitwise_xor(irreps, sym)]
            term = jnp.einsum('gpad,gpbd->gab', half_step.astype(jnp.float32), chol_sel)
            return totals + term, None

        totals, unused = lax.scan(per_aux, jnp.zeros((IRREPS, WB, WB), jnp.float32), irreps)
        return totals

    flat = amplitudes.reshape(NOCC * NOCC, IRREPS, VB, VB)
    ladder = lax.map(one_pair, (flat, pair_irrep.reshape(NOCC * NOCC)))
    ladder = ladder.reshape(NOCC, NOCC, IRREPS, WB, WB)
    turned = jnp.transpose(ladder, (1, 0, 2, 4, 3))
    picks = jnp.bitwise_xor(irreps[None, None, :], pair_irrep[:, :, None]).astype(jnp.int32)
    partner = jnp.take_along_axis(turned, picks[:, :, :, None, None], axis=2)
    return ladder + partner
```

```python
import jax
import jax.numpy as jnp
from jax import lax
from jax.experimental import pallas as pl
from jax.experimental.pallas import tpu as pltpu
from jax.sharding import PartitionSpec as P

IRREPS = 8
VB = 128
PB = 256
WB = 4
LO = 8
HI = VB // LO
PAIRS = 32
COLS = PAIRS * LO
AXES = ("oi", "oj", "vert")
CHIPS = [
    (x, zh, core, zl, y)
    for x in range(4)
    for zh in range(4)
    for core in range(2)
    for zl in range(2)
    for y in range(4)
]
NT = (((1,), (1,)), ((), ()))


def flat_index(x, zh, core, zl, y):
    return x * 64 + (zh * 2 + core) * 8 + zl * 4 + y


def fetch_pairs(rz, ry):
    pairs = []
    for x, zh, core, zl, y in CHIPS:
        source = (x, (zh + y + 2 * zl) % 4, zl, core ^ rz, y ^ ry)
        pairs.append((flat_index(*source), flat_index(x, zh, core, zl, y)))
    return pairs


def across_pairs():
    pairs = []
    for x, zh, core, zl, y in CHIPS:
        step = 1 if core else -1
        pairs.append((flat_index(x, zh, core, zl, y), flat_index((x + step) % 4, zh, core, zl, y)))
    return pairs


def swap_pairs():
    return [(flat_index(*d), flat_index(d[0], d[1], 1 - d[2], d[3], d[4])) for d in CHIPS]


def mirror_pairs(k):
    pairs = []
    for x in range(4):
        for col in range(8):
            target = (col // 2) * 8 + 2 * x + (k ^ (col % 2))
            pairs.append((x * 8 + col, target))
    return pairs


def spread_kernel(amp_ref, out_ref):
    wide = amp_ref[:, 0].astype(jnp.float32).reshape(PAIRS, HI, LO, VB)
    for hi in range(HI):
        out_ref[0, :, hi * VB : (hi + 1) * VB] = (
            wide[:, hi].reshape(COLS, VB).astype(jnp.bfloat16)
        )


def spread(amplitudes):
    return pl.pallas_call(
        spread_kernel,
        out_shape=jax.ShapeDtypeStruct((IRREPS, COLS, HI * VB), jnp.bfloat16),
        grid=(IRREPS,),
        in_specs=[pl.BlockSpec((PAIRS, 1, VB, VB), lambda g: (0, g, 0, 0))],
        out_specs=pl.BlockSpec((1, COLS, HI * VB), lambda g: (g, 0, 0)),
        compiler_params=pltpu.CompilerParams(vmem_limit_bytes=24 * 2**20),
        cost_estimate=pl.CostEstimate(flops=0, bytes_accessed=2**24, transcendentals=0),
    )(amplitudes)


def ladder_kernel(
    flip_ref, place_ref, *refs
):
    pieces = refs[:8]
    amp_ref, sym_ref, own_sel_ref, mirror_sel_ref, own_ref, mirror_ref = refs[8:14]
    chol, window, turned, sem = refs[14:]
    step = pl.program_id(0)

    @pl.when(step == 0)
    def _():
        copies = []
        for at in range(8):
            for ry in range(4):
                copies.append(
                    pltpu.make_async_copy(
                        pieces[at].at[ry],
                        chol.at[place_ref[2 * at] * 4 + ry, place_ref[2 * at + 1]],
                        sem.at[at * 4 + ry],
                    )
                )
        for copy in copies:
            copy.start()
        for copy in copies:
            copy.wait()
        turned[...] = jnp.zeros_like(turned)

    left = chol[step].reshape(WB * VB, PB)
    for gb in range(IRREPS):
        for half in range(2):
            right = chol[gb, 2 * half : 2 * half + 2].reshape(2 * VB, PB)
            block = lax.dot_general(left, right, NT, preferred_element_type=jnp.float32)
            for a in range(WB):
                base = ((gb * WB + a) * WB + 2 * half) * LO
                for hi in range(HI):
                    row = a * VB + hi * LO
                    window[base : base + 2 * LO, hi * VB : (hi + 1) * VB] = jnp.concatenate(
                        [block[row : row + LO, :VB], block[row : row + LO, VB:]], 0
                    ).astype(jnp.bfloat16)

    full = lax.dot_general(window[...], amp_ref[0], NT, preferred_element_type=jnp.float32)
    full = full.reshape(IRREPS * WB * WB, LO, COLS)
    lo_row = lax.broadcasted_iota(jnp.int32, (LO, COLS), 0)
    lo_col = lax.broadcasted_iota(jnp.int32, (LO, COLS), 1)
    full = jnp.where((lo_col % LO == lo_row)[None], full, 0.0)
    sums = jnp.sum(full, axis=1).reshape(IRREPS, WB * WB, COLS)
    irrep = lax.broadcasted_iota(jnp.int32, (IRREPS, 1, COLS), 0)
    wanted = jnp.bitwise_xor(sym_ref[...], step)[None]
    sums = jnp.where(irrep == wanted, sums, 0.0)
    turned[...] += sums

    row = lax.broadcasted_iota(jnp.int32, (WB * WB, VB), 0)
    group = lax.broadcasted_iota(jnp.int32, (WB * WB, VB), 1) // PAIRS
    own = jnp.dot(
        jnp.sum(sums, axis=0),
        own_sel_ref[...],
        preferred_element_type=jnp.float32,
        precision=lax.Precision.HIGHEST,
    )
    own = jnp.where(group == row % WB, own, 0.0)
    own_ref[0] = jnp.sum(own.reshape(WB, WB, VB), axis=1)

    @pl.when(step == IRREPS - 1)
    def _():
        every = turned[...].reshape(IRREPS * WB * WB, COLS)
        for k in range(2):
            other = jnp.dot(
                every,
                mirror_sel_ref[k],
                preferred_element_type=jnp.float32,
                precision=lax.Precision.HIGHEST,
            ).reshape(IRREPS, WB * WB, VB)
            other = jnp.where((group == row // WB)[None], other, 0.0)
            mirror_ref[k] = jnp.sum(other.reshape(IRREPS, WB, WB, VB), axis=1)


def ladder(flip, place, pieces, amp, sym, own_sel, mirror_sel):
    anywhere = pl.BlockSpec(memory_space=pl.ANY)
    return pl.pallas_call(
        ladder_kernel,
        out_shape=[
            jax.ShapeDtypeStruct((IRREPS, WB, VB), jnp.float32),
            jax.ShapeDtypeStruct((2, IRREPS, WB, VB), jnp.float32),
        ],
        grid_spec=pltpu.PrefetchScalarGridSpec(
            num_scalar_prefetch=2,
            grid=(IRREPS,),
            in_specs=[anywhere] * 8
            + [
                pl.BlockSpec((1, COLS, HI * VB), lambda g, flip, place: (g ^ flip[0], 0, 0)),
                pl.BlockSpec((1, COLS), lambda g, flip, place: (0, 0)),
                pl.BlockSpec((COLS, VB), lambda g, flip, place: (0, 0)),
                pl.BlockSpec((2, COLS, VB), lambda g, flip, place: (0, 0, 0)),
            ],
            out_specs=[
                pl.BlockSpec((1, WB, VB), lambda g, flip, place: (g, 0, 0)),
                pl.BlockSpec((2, IRREPS, WB, VB), lambda g, flip, place: (0, 0, 0, 0)),
            ],
            scratch_shapes=[
                pltpu.VMEM((IRREPS, WB, VB, PB), jnp.bfloat16),
                pltpu.VMEM((IRREPS * WB * WB * LO, HI * VB), jnp.bfloat16),
                pltpu.VMEM((IRREPS, WB * WB, COLS), jnp.float32),
                pltpu.SemaphoreType.DMA((32,)),
            ],
        ),
        compiler_params=pltpu.CompilerParams(vmem_limit_bytes=40 * 2**20),
        cost_estimate=pl.CostEstimate(flops=2 * 8 * 10**9, bytes_accessed=12 * 10**6, transcendentals=0),
    )(flip, place, *pieces, amp, sym, own_sel, mirror_sel)


def local(amplitudes, chol, occ_irrep):
    x = lax.axis_index("oi")
    oj = lax.axis_index("oj")
    vert = lax.axis_index("vert")
    zh, core, zl, y = oj // 2, oj % 2, vert // 4, vert % 4
    even = x % 2

    def permute(value, pairs):
        return lax.ppermute(value, AXES, pairs)

    own = jnp.transpose(chol[0], (1, 2, 0))
    quarters = [lax.dynamic_index_in_dim(own, 2 * even + (zl ^ rz), 0, False) for rz in range(2)]
    pieces, place = [], []
    for rz in range(2):
        near = jnp.stack([permute(quarters[rz], fetch_pairs(rz, ry)) for ry in range(4)])
        far = permute(near, across_pairs())
        pieces += [near, far, permute(near, swap_pairs()), permute(far, swap_pairs())]
        first = core ^ rz ^ zl
        place += [first, 2 * even + core, first, 2 * (1 - even) + core]
        place += [1 - first, 2 * even + 1 - core, 1 - first, 2 * (1 - even) + 1 - core]
    place = jnp.stack(place).astype(jnp.int32)

    block = ((zh + y + 2 * zl) % 4) * 2 + zl
    flip = (block ^ vert).astype(jnp.int32)[None]
    occ_rows, occ_cols = amplitudes.shape[0], amplitudes.shape[1]
    irrep_rows = lax.dynamic_slice_in_dim(occ_irrep, x * occ_rows, occ_rows)
    irrep_cols = lax.dynamic_slice_in_dim(occ_irrep, oj * occ_cols, occ_cols)
    sym = jnp.bitwise_xor(irrep_rows[:, None], irrep_cols[None, :])
    sym = jnp.broadcast_to(sym.reshape(1, PAIRS, 1), (1, PAIRS, LO)).reshape(1, COLS)

    pair = jnp.arange(COLS, dtype=jnp.int32)[:, None] // LO
    lane = jnp.arange(VB, dtype=jnp.int32)[None, :] % PAIRS
    own_sel = (pair == lane).astype(jnp.float32)
    row, col = pair // occ_cols, pair % occ_cols
    spot = core * 16 + col * 4 + row % 4
    mirror_sel = jnp.stack(
        [((lane == spot) & (row // 4 == (core ^ k))).astype(jnp.float32) for k in range(2)]
    )

    amp = spread(amplitudes.reshape(PAIRS, IRREPS, VB, VB))
    mine, other = ladder(flip, place, pieces, amp, sym, own_sel, mirror_sel)
    total = mine
    for k in range(2):
        total = total + lax.ppermute(other[k], ("oi", "oj"), mirror_pairs(k))
    for bit in (4, 2, 1):
        pairs = [(v, v ^ bit) for v in range(IRREPS)]
        total = total[:bit] + lax.ppermute(total[bit:], "vert", pairs)
    total = total.reshape(WB, WB, occ_rows, occ_cols)
    return jnp.transpose(total, (2, 3, 0, 1))[:, :, None]


def solution(mesh):
    return jax.shard_map(
        local,
        mesh=mesh,
        in_specs=(P("oi", "oj", None, None, None), P(("oj", "vert"), None, None, None), P()),
        out_specs=P("oi", "oj", "vert", None, None),
        check_vma=False,
    )
```

```python
import jax
import jax.numpy as jnp
from jax import lax
from jax.experimental import pallas as pl
from jax.experimental.pallas import tpu as pltpu
from jax.sharding import PartitionSpec as P

IRREPS = 8
VB = 128
PB = 256
WB = 4
LO = 8
HI = VB // LO
PAIRS = 32
COLS = PAIRS * LO
AXES = ("oi", "oj", "vert")
CHIPS = [
    (x, zh, core, zl, y)
    for x in range(4)
    for zh in range(4)
    for core in range(2)
    for zl in range(2)
    for y in range(4)
]
NT = (((1,), (1,)), ((), ()))


def flat_index(x, zh, core, zl, y):
    return x * 64 + (zh * 2 + core) * 8 + zl * 4 + y


def fetch_pairs(far):
    pairs = []
    for x, zh, core, zl, y in CHIPS:
        source = (x, (zh + y + 2 * zl) % 4, zl, core, y ^ (2 * far))
        pairs.append((flat_index(*source), flat_index(x, zh, core, zl, y)))
    return pairs


def moved_pairs(move):
    return [(flat_index(*d), flat_index(*move(*d))) for d in CHIPS]


def next_row(x, zh, core, zl, y):
    return (x, zh, core, zl, y ^ 1)


def lower(x, zh, core, zl, y):
    return ((x + 3) % 4, zh, core, zl, y)


def upper(x, zh, core, zl, y):
    return ((x + 1) % 4, zh, core, zl, y)


def apart(x, zh, core, zl, y):
    return ((x + (1 if core else 3)) % 4, zh, core, zl, y)


def other_core(x, zh, core, zl, y):
    return (x, zh, 1 - core, zl, y)


def mirrored(x, zh, core, zl, y):
    return (zh, x, core, zl, y)


def ladder_kernel(
    flip_ref, place_ref, *refs
):
    pieces = refs[:8]
    amp_ref, sym_ref, own_sel_ref, mirror_sel_ref, own_ref, mirror_ref = refs[8:14]
    chol, window, spread, turned, sem = refs[14:]
    step = pl.program_id(0)

    @pl.when(step == 0)
    def _():
        copies = []
        for at in range(8):
            for ry in range(4):
                copies.append(
                    pltpu.make_async_copy(
                        pieces[at].at[ry],
                        chol.at[place_ref[2 * at] * 4 + ry, place_ref[2 * at + 1]],
                        sem.at[at * 4 + ry],
                    )
                )
        for copy in copies:
            copy.start()
        for copy in copies:
            copy.wait()
        turned[...] = jnp.zeros_like(turned)

    wide = amp_ref[:, 0].astype(jnp.float32).reshape(PAIRS, HI, LO, VB)
    for hi in range(HI):
        spread[:, hi * VB : (hi + 1) * VB] = wide[:, hi].reshape(COLS, VB).astype(jnp.bfloat16)

    left = chol[step].reshape(WB * VB, PB)
    for gb in range(IRREPS):
        for half in range(2):
            right = chol[gb, 2 * half : 2 * half + 2].reshape(2 * VB, PB)
            block = lax.dot_general(left, right, NT, preferred_element_type=jnp.float32)
            for a in range(WB):
                base = ((gb * WB + a) * WB + 2 * half) * LO
                for hi in range(HI):
                    row = a * VB + hi * LO
                    window[base : base + 2 * LO, hi * VB : (hi + 1) * VB] = jnp.concatenate(
                        [block[row : row + LO, :VB], block[row : row + LO, VB:]], 0
                    ).astype(jnp.bfloat16)

    full = lax.dot_general(window[...], spread[...], NT, preferred_element_type=jnp.float32)
    full = full.reshape(IRREPS * WB * WB, LO, COLS)
    lo_row = lax.broadcasted_iota(jnp.int32, (LO, COLS), 0)
    lo_col = lax.broadcasted_iota(jnp.int32, (LO, COLS), 1)
    full = jnp.where((lo_col % LO == lo_row)[None], full, 0.0)
    sums = jnp.sum(full, axis=1).reshape(IRREPS, WB * WB, COLS)
    irrep = lax.broadcasted_iota(jnp.int32, (IRREPS, 1, COLS), 0)
    wanted = jnp.bitwise_xor(sym_ref[...], step)[None]
    sums = jnp.where(irrep == wanted, sums, 0.0)
    turned[...] += sums

    row = lax.broadcasted_iota(jnp.int32, (WB * WB, VB), 0)
    group = lax.broadcasted_iota(jnp.int32, (WB * WB, VB), 1) // PAIRS
    own = jnp.dot(
        jnp.sum(sums, axis=0),
        own_sel_ref[...],
        preferred_element_type=jnp.float32,
        precision=lax.Precision.HIGHEST,
    )
    own = jnp.where(group == row % WB, own, 0.0)
    own_ref[0] = jnp.sum(own.reshape(WB, WB, VB), axis=1)

    @pl.when(step == IRREPS - 1)
    def _():
        every = turned[...].reshape(IRREPS * WB * WB, COLS)
        for k in range(2):
            other = jnp.dot(
                every,
                mirror_sel_ref[k],
                preferred_element_type=jnp.float32,
                precision=lax.Precision.HIGHEST,
            ).reshape(IRREPS, WB * WB, VB)
            other = jnp.where((group == row // WB)[None], other, 0.0)
            mirror_ref[k] = jnp.sum(other.reshape(IRREPS, WB, WB, VB), axis=1)


def ladder(flip, place, pieces, amp, sym, own_sel, mirror_sel):
    anywhere = pl.BlockSpec(memory_space=pl.ANY)
    return pl.pallas_call(
        ladder_kernel,
        out_shape=[
            jax.ShapeDtypeStruct((IRREPS, WB, VB), jnp.float32),
            jax.ShapeDtypeStruct((2, IRREPS, WB, VB), jnp.float32),
        ],
        grid_spec=pltpu.PrefetchScalarGridSpec(
            num_scalar_prefetch=2,
            grid=(IRREPS,),
            in_specs=[anywhere] * 8
            + [
                pl.BlockSpec((PAIRS, 1, VB, VB), lambda g, flip, place: (0, g ^ flip[0], 0, 0)),
                pl.BlockSpec((1, COLS), lambda g, flip, place: (0, 0)),
                pl.BlockSpec((COLS, VB), lambda g, flip, place: (0, 0)),
                pl.BlockSpec((2, COLS, VB), lambda g, flip, place: (0, 0, 0)),
            ],
            out_specs=[
                pl.BlockSpec((1, WB, VB), lambda g, flip, place: (g, 0, 0)),
                pl.BlockSpec((2, IRREPS, WB, VB), lambda g, flip, place: (0, 0, 0, 0)),
            ],
            scratch_shapes=[
                pltpu.VMEM((IRREPS, WB, VB, PB), jnp.bfloat16),
                pltpu.VMEM((IRREPS * WB * WB * LO, HI * VB), jnp.bfloat16),
                pltpu.VMEM((COLS, HI * VB), jnp.bfloat16),
                pltpu.VMEM((IRREPS, WB * WB, COLS), jnp.float32),
                pltpu.SemaphoreType.DMA((32,)),
            ],
        ),
        compiler_params=pltpu.CompilerParams(vmem_limit_bytes=52 * 2**20),
        cost_estimate=pl.CostEstimate(flops=2 * 8 * 10**9, bytes_accessed=12 * 10**6, transcendentals=0),
    )(flip, place, *pieces, amp, sym, own_sel, mirror_sel)


def local(amplitudes, chol, occ_irrep):
    x = lax.axis_index("oi")
    oj = lax.axis_index("oj")
    vert = lax.axis_index("vert")
    zh, core, zl, y = oj // 2, oj % 2, vert // 4, vert % 4

    def permute(value, pairs):
        return lax.ppermute(value, AXES, pairs)

    mine = lax.dynamic_index_in_dim(chol[0], x, 1, False).T
    pair = jnp.stack([mine, permute(mine, moved_pairs(next_row))])
    near = jnp.concatenate([permute(pair, fetch_pairs(far)) for far in range(2)])
    above, below = permute(near, moved_pairs(lower)), permute(near, moved_pairs(upper))
    opposite = permute(jnp.where(core == 0, above, below), moved_pairs(apart))
    pieces, place = [], []
    for hop, piece in ((0, near), (1, above), (3, below), (2, opposite)):
        first, a = core ^ zl, (x + hop) % 4
        pieces += [piece, permute(piece, moved_pairs(other_core))]
        place += [first, a, 1 - first, a]
    place = jnp.stack(place).astype(jnp.int32)

    block = ((zh + y + 2 * zl) % 4) * 2 + zl
    flip = (block ^ vert).astype(jnp.int32)[None]
    occ_rows, occ_cols = amplitudes.shape[0], amplitudes.shape[1]
    irrep_rows = lax.dynamic_slice_in_dim(occ_irrep, x * occ_rows, occ_rows)
    irrep_cols = lax.dynamic_slice_in_dim(occ_irrep, oj * occ_cols, occ_cols)
    sym = jnp.bitwise_xor(irrep_rows[:, None], irrep_cols[None, :])
    sym = jnp.broadcast_to(sym.reshape(1, PAIRS, 1), (1, PAIRS, LO)).reshape(1, COLS)

    pair = jnp.arange(COLS, dtype=jnp.int32)[:, None] // LO
    lane = jnp.arange(VB, dtype=jnp.int32)[None, :] % PAIRS
    own_sel = (pair == lane).astype(jnp.float32)
    row, col = pair // occ_cols, pair % occ_cols
    spot = core * 16 + col * 4 + row % 4
    mirror_sel = jnp.stack(
        [((lane == spot) & (row // 4 == (core ^ k))).astype(jnp.float32) for k in range(2)]
    )

    amp = amplitudes.reshape(PAIRS, IRREPS, VB, VB)
    mine, other = ladder(flip, place, pieces, amp, sym, own_sel, mirror_sel)
    other = other[0] + permute(other[1], moved_pairs(other_core))
    total = mine + permute(other, moved_pairs(mirrored))
    for bit in (4, 2, 1):
        pairs = [(v, v ^ bit) for v in range(IRREPS)]
        total = total[:bit] + lax.ppermute(total[bit:], "vert", pairs)
    total = total.reshape(WB, WB, occ_rows, occ_cols)
    return jnp.transpose(total, (2, 3, 0, 1))[:, :, None]


def solution(mesh):
    return jax.shard_map(
        local,
        mesh=mesh,
        in_specs=(P("oi", "oj", None, None, None), P(("oj", "vert"), None, None, None), P()),
        out_specs=P("oi", "oj", "vert", None, None),
        check_vma=False,
    )
```

```python
import jax
import jax.numpy as jnp
from jax import lax
from jax.experimental import pallas as pl
from jax.experimental.pallas import tpu as pltpu
from jax.sharding import PartitionSpec as P

IRREPS = 8
VB = 128
PB = 256
WB = 4
LO = 8
HI = VB // LO
PAIRS = 32
HOPS = (0, 1, 3, 2)
COLS = PAIRS * LO
AXES = ("oi", "oj", "vert")
CHIPS = [
    (x, zh, core, zl, y)
    for x in range(4)
    for zh in range(4)
    for core in range(2)
    for zl in range(2)
    for y in range(4)
]
NT = (((1,), (1,)), ((), ()))


def flat_index(x, zh, core, zl, y):
    return x * 64 + (zh * 2 + core) * 8 + zl * 4 + y


def fetch_pairs(row):
    pairs = []
    for x, zh, core, zl, y in CHIPS:
        source = (x, (zh + y + 2 * zl) % 4, zl, core, y ^ row)
        pairs.append((flat_index(*source), flat_index(x, zh, core, zl, y)))
    return pairs


def moved_pairs(move):
    return [(flat_index(*d), flat_index(*move(*d))) for d in CHIPS]


def lower(x, zh, core, zl, y):
    return ((x + 3) % 4, zh, core, zl, y)


def upper(x, zh, core, zl, y):
    return ((x + 1) % 4, zh, core, zl, y)


def apart(x, zh, core, zl, y):
    return ((x + (1 if core else 3)) % 4, zh, core, zl, y)


def other_core(x, zh, core, zl, y):
    return (x, zh, 1 - core, zl, y)


def mirrored(x, zh, core, zl, y):
    return (zh, x, core, zl, y)


def exact_pick(values, chosen):
    top = values.astype(jnp.bfloat16)
    rest = values - top.astype(jnp.float32)
    middle = rest.astype(jnp.bfloat16)
    low = (rest - middle.astype(jnp.float32)).astype(jnp.bfloat16)
    rows = values.shape[0]
    parts = jnp.dot(
        jnp.concatenate([top, middle, low], 0), chosen, preferred_element_type=jnp.float32
    )
    return parts[:rows] + (parts[rows : 2 * rows] + parts[2 * rows :])


def place_of():
    x, oj, vert = lax.axis_index("oi"), lax.axis_index("oj"), lax.axis_index("vert")
    zh, core, zl, y = oj // 2, lax.rem(oj, 2), vert // 4, lax.rem(vert, 4)
    block = lax.rem(zh + y + 2 * zl, 4) * 2 + zl
    return x, oj, vert, core, jnp.bitwise_xor(block, vert), jnp.bitwise_xor(core, zl)


def load_pieces(pieces, chol, sems, first):
    copies = []
    for at, piece in enumerate(pieces):
        half = first if at % 2 == 0 else 1 - first
        target = chol.at[pl.ds(half * 4, 4), at // 2]
        copies.append(pltpu.make_async_copy(piece, target, sems.at[at]))
    return copies


def pair_labels(occ, x, oj):
    pair = lax.broadcasted_iota(jnp.int32, (1, COLS), 1) // LO
    sym = jnp.zeros((1, COLS), jnp.int32)
    for row in range(8):
        for col in range(4):
            label = jnp.bitwise_xor(occ[x * 8 + row], occ[oj * 4 + col])
            sym = jnp.where(pair == row * 4 + col, label, sym)
    lo_row = lax.broadcasted_iota(jnp.int32, (LO, COLS), 0)
    lo_col = lax.broadcasted_iota(jnp.int32, (LO, COLS), 1) % LO
    return jnp.where(lo_row == lo_col, sym, -1)


def store_block(window, base, block, row):
    for hi in range(HI):
        at = row + hi * LO
        window[base : base + 2 * LO, hi * VB : (hi + 1) * VB] = jnp.concatenate(
            [block[at : at + LO, :VB], block[at : at + LO, VB:]], 0
        ).astype(jnp.bfloat16)


def spread_out(amp, spread):
    wide = amp.astype(jnp.float32).reshape(PAIRS, HI, LO, VB)
    for hi in range(HI):
        spread[:, hi * VB : (hi + 1) * VB] = wide[:, hi].reshape(COLS, VB).astype(jnp.bfloat16)


def collect(full, sym, ga, where, straight, turned):
    totals = {}
    for at, (gb, a, b) in enumerate(where):
        wanted = sym == jnp.bitwise_xor(ga, gb)
        slot = WB * a + b
        totals[slot] = jnp.where(wanted, full[at], totals.get(slot, 0.0))
        turned[gb, slot] = jnp.where(wanted, full[at], turned[gb, slot])
    for slot, total in totals.items():
        straight[ga, slot] = total


def finish(slots, straight, turned, own_ref, mirror_ref, x, core, vert):
    count = len(slots)
    actual = [lax.rem(x + hop, WB) for hop in HOPS]
    source = lax.broadcasted_iota(jnp.int32, (COLS, VB), 0) // LO
    lane = lax.broadcasted_iota(jnp.int32, (COLS, VB), 1) % PAIRS
    group = lax.broadcasted_iota(jnp.int32, (IRREPS, VB), 1) // PAIRS

    def summed(values):
        rows = [jnp.sum(values[:, WB * a + b], axis=1) for a, b in slots]
        return jnp.concatenate(rows, 0)

    def split(values, chosen, by_first):
        picked = exact_pick(values, chosen)
        lines = {}
        for at, (a, b) in enumerate(slots):
            line, wide = (a, b) if by_first else (b, a)
            part = jnp.where(group == actual[wide], picked[at * IRREPS : (at + 1) * IRREPS], 0.0)
            lines[line] = lines.get(line, 0.0) + part
        return lines

    own = split(summed(straight), (source == lane).astype(jnp.bfloat16), True)
    for line, value in own.items():
        for ga in range(IRREPS):
            there = (jnp.bitwise_xor(vert, ga), pl.ds(actual[line], 1))
            own_ref[there] = own_ref[there] + value[ga : ga + 1]
    every = summed(turned)
    target = core * 16 + (source % 4) * 4 + (source // 4) % 4
    for k in range(2):
        here = (source // 16) == jnp.bitwise_xor(core, k)
        other = split(every, ((lane == target) & here).astype(jnp.bfloat16), False)
        for line, value in other.items():
            for ga in range(IRREPS):
                there = (k, jnp.bitwise_xor(vert, ga), pl.ds(actual[line], 1))
                mirror_ref[there] = mirror_ref[there] + value[ga : ga + 1]


def amp_copy(amp_ref, amp, sems, flip, ga):
    return pltpu.make_async_copy(
        amp_ref.at[:, jnp.bitwise_xor(ga, flip)], amp.at[ga], sems.at[ga]
    )


def begin(occ_ref, amp_ref, pieces, chol, amp, occ, sems, flip, first):
    chol_sem, amp_sem, occ_sem = sems
    occ_copy = pltpu.make_async_copy(occ_ref, occ, occ_sem)
    occ_copy.start()
    amp_copy(amp_ref, amp, amp_sem, flip, 0).start()
    copies = load_pieces(pieces, chol, chol_sem, first)
    for copy in copies:
        copy.start()
    occ_copy.wait()
    for copy in copies:
        copy.wait()
    for ga in range(1, IRREPS):
        amp_copy(amp_ref, amp, amp_sem, flip, ga).start()


def early_kernel(occ_ref, amp_ref, *refs):
    pieces, (own_ref, mirror_ref) = refs[:6], refs[6:8]
    chol, amp, window, spread, straight, turned, occ, *sems = refs[8:]
    x, oj, vert, core, flip, first = place_of()
    begin(occ_ref, amp_ref, pieces, chol, amp, occ, sems, flip, first)
    sym = pair_labels(occ, x, oj)
    where = []
    for tile in range(12):
        for a in range(3):
            for at in (2 * tile, 2 * tile + 1):
                where.append((at // 3, a, at % 3))
    slots = [(a, b) for a in range(3) for b in range(3)]
    for a, b in slots:
        turned[:, WB * a + b] = jnp.zeros((IRREPS, LO, COLS), jnp.float32)
    own_ref[...] = jnp.zeros_like(own_ref)
    mirror_ref[...] = jnp.zeros_like(mirror_ref)

    def one_irrep(ga, carry):
        amp_copy(amp_ref, amp, sems[1], flip, ga).wait()
        spread_out(amp[ga], spread)
        left = chol[ga].reshape(3 * VB, PB)
        for tile in range(12):
            two = [chol[at // 3, at % 3] for at in (2 * tile, 2 * tile + 1)]
            block = lax.dot_general(
                left, jnp.concatenate(two, 0), NT, preferred_element_type=jnp.float32
            )
            for a in range(3):
                store_block(window, (tile * 3 + a) * 2 * LO, block, a * VB)
        full = []
        for start, stop in ((0, 32), (32, 72)):
            rows = window[start * LO : stop * LO]
            part = lax.dot_general(rows, spread[...], NT, preferred_element_type=jnp.float32)
            full.append(part.reshape(stop - start, LO, COLS))
        collect(jnp.concatenate(full, 0), sym, ga, where, straight, turned)
        return carry

    lax.fori_loop(0, IRREPS, one_irrep, 0)
    finish(slots, straight, turned, own_ref, mirror_ref, x, core, vert)


def late_kernel(occ_ref, amp_ref, own_in, mirror_in, *refs):
    pieces, (own_ref, mirror_ref) = refs[:8], refs[8:10]
    chol, amp, window, spread, straight, turned, occ, *sems = refs[10:]
    x, oj, vert, core, flip, first = place_of()
    begin(occ_ref, amp_ref, pieces, chol, amp, occ, sems, flip, first)
    sym = pair_labels(occ, x, oj)
    where = []
    for tile in range(4):
        for a in range(4):
            where += [(2 * tile, a, 3), (2 * tile + 1, a, 3)]
    for at in range(24):
        where.append((at // 3, 3, at % 3))
    slots = [(a, 3) for a in range(4)] + [(3, b) for b in range(3)]
    for a, b in slots:
        turned[:, WB * a + b] = jnp.zeros((IRREPS, LO, COLS), jnp.float32)
    own_ref[...] = own_in[...]
    mirror_ref[...] = mirror_in[...]

    def one_irrep(ga, carry):
        amp_copy(amp_ref, amp, sems[1], flip, ga).wait()
        spread_out(amp[ga], spread)
        left = chol[ga].reshape(WB * VB, PB)
        for tile in range(4):
            two = [chol[2 * tile, 3], chol[2 * tile + 1, 3]]
            block = lax.dot_general(
                left, jnp.concatenate(two, 0), NT, preferred_element_type=jnp.float32
            )
            for a in range(WB):
                store_block(window, (tile * WB + a) * 2 * LO, block, a * VB)
        for tile in range(12):
            two = [chol[at // 3, at % 3] for at in (2 * tile, 2 * tile + 1)]
            block = lax.dot_general(
                chol[ga, 3], jnp.concatenate(two, 0), NT, preferred_element_type=jnp.float32
            )
            store_block(window, (16 + tile) * 2 * LO, block, 0)
        for start, stop in ((0, 32), (32, 56)):
            rows = window[start * LO : stop * LO]
            part = lax.dot_general(rows, spread[...], NT, preferred_element_type=jnp.float32)
            part = part.reshape(stop - start, LO, COLS)
            collect(part, sym, ga, where[start:stop], straight, turned)
        return carry

    lax.fori_loop(0, IRREPS, one_irrep, 0)
    finish(slots, straight, turned, own_ref, mirror_ref, x, core, vert)


def ladder(kernel, slots, window, before, pieces):
    anywhere = pl.BlockSpec(memory_space=pl.ANY)
    whole = pl.BlockSpec(memory_space=pltpu.VMEM)
    occ, amp, *earlier = before
    return pl.pallas_call(
        kernel,
        out_shape=[
            jax.ShapeDtypeStruct((IRREPS, WB, VB), jnp.float32),
            jax.ShapeDtypeStruct((2, IRREPS, WB, VB), jnp.float32),
        ],
        in_specs=[anywhere] * 2 + [whole] * len(earlier) + [anywhere] * len(pieces),
        out_specs=[whole] * 2,
        scratch_shapes=[
            pltpu.VMEM((IRREPS, slots, VB, PB), jnp.bfloat16),
            pltpu.VMEM((IRREPS, PAIRS, VB, VB), jnp.bfloat16),
            pltpu.VMEM(window + (HI * VB,), jnp.bfloat16),
            pltpu.VMEM((COLS, HI * VB), jnp.bfloat16),
            pltpu.VMEM((IRREPS, WB * WB, LO, COLS), jnp.float32),
            pltpu.VMEM((IRREPS, WB * WB, LO, COLS), jnp.float32),
            pltpu.SMEM((PAIRS,), jnp.int32),
            pltpu.SemaphoreType.DMA((8,)),
            pltpu.SemaphoreType.DMA((8,)),
            pltpu.SemaphoreType.DMA,
        ],
        compiler_params=pltpu.CompilerParams(vmem_limit_bytes=50 * 2**20),
        cost_estimate=pl.CostEstimate(
            flops=8 * 10**9, bytes_accessed=12 * 10**6, transcendentals=0
        ),
    )(*before, *pieces)


def local(amplitudes, chol, occ_irrep):
    x = lax.axis_index("oi")
    core = lax.rem(lax.axis_index("oj"), 2)

    def permute(value, pairs):
        return lax.ppermute(value, AXES, pairs)

    mine = lax.dynamic_index_in_dim(chol[0], x, 1, False).T
    near = jnp.stack([permute(mine, fetch_pairs(row)) for row in range(4)])
    above, below = permute(near, moved_pairs(lower)), permute(near, moved_pairs(upper))
    pieces = []
    for piece in (near, above, below):
        pieces += [piece, permute(piece, moved_pairs(other_core))]
    beyond = jnp.where(core == 0, jnp.stack(pieces[2:4]), jnp.stack(pieces[4:6]))
    beyond = permute(beyond, moved_pairs(apart))
    occ_rows, occ_cols = amplitudes.shape[0], amplitudes.shape[1]
    amp = amplitudes.reshape(PAIRS, IRREPS, VB, VB)
    before = (occ_irrep, amp)
    mine, other = ladder(early_kernel, 3, (72 * LO,), before, pieces)
    before += (mine, other)
    pieces += [beyond[0], beyond[1]]
    mine, other = ladder(late_kernel, 4, (56 * LO,), before, pieces)
    other = other[0] + permute(other[1], moved_pairs(other_core))
    total = mine + permute(other, moved_pairs(mirrored))
    total = jnp.sum(lax.all_to_all(total, "vert", 0, 0), axis=0)
    total = total.reshape(WB, WB, occ_rows, occ_cols)
    return jnp.transpose(total, (2, 3, 0, 1))[:, :, None]


def solution(mesh):
    return jax.shard_map(
        local,
        mesh=mesh,
        in_specs=(P("oi", "oj", None, None, None), P(("oj", "vert"), None, None, None), P()),
        out_specs=P("oi", "oj", "vert", None, None),
        check_vma=False,
    )
```

```python
import jax
import jax.numpy as jnp
from jax import lax
from jax.experimental import pallas as pl
from jax.experimental.pallas import tpu as pltpu
from jax.sharding import PartitionSpec as P

IRREPS = 8
VB = 128
PB = 256
WB = 4
LO = 8
HI = VB // LO
PAIRS = 32
HOPS = (0, 1, 3, 2)
COLS = PAIRS * LO
AXES = ("oi", "oj", "vert")
CHIPS = [
    (x, zh, core, zl, y)
    for x in range(4)
    for zh in range(4)
    for core in range(2)
    for zl in range(2)
    for y in range(4)
]
NT = (((1,), (1,)), ((), ()))


def flat_index(x, zh, core, zl, y):
    return x * 64 + (zh * 2 + core) * 8 + zl * 4 + y


def fetch_pairs(row):
    pairs = []
    for x, zh, core, zl, y in CHIPS:
        source = (x, (zh + y + 2 * zl) % 4, zl, core, y ^ row)
        pairs.append((flat_index(*source), flat_index(x, zh, core, zl, y)))
    return pairs


def moved_pairs(move):
    return [(flat_index(*d), flat_index(*move(*d))) for d in CHIPS]


def lower(x, zh, core, zl, y):
    return ((x + 3) % 4, zh, core, zl, y)


def upper(x, zh, core, zl, y):
    return ((x + 1) % 4, zh, core, zl, y)


def apart(x, zh, core, zl, y):
    return ((x + (1 if core else 3)) % 4, zh, core, zl, y)


def other_core(x, zh, core, zl, y):
    return (x, zh, 1 - core, zl, y)


def mirrored(x, zh, core, zl, y):
    return (zh, x, core, zl, y)


def exact_pick(values, chosen):
    top = values.astype(jnp.bfloat16)
    rest = values - top.astype(jnp.float32)
    middle = rest.astype(jnp.bfloat16)
    low = (rest - middle.astype(jnp.float32)).astype(jnp.bfloat16)
    rows = values.shape[0]
    parts = jnp.dot(
        jnp.concatenate([top, middle, low], 0), chosen, preferred_element_type=jnp.float32
    )
    return parts[:rows] + (parts[rows : 2 * rows] + parts[2 * rows :])


def place_of():
    x, oj, vert = lax.axis_index("oi"), lax.axis_index("oj"), lax.axis_index("vert")
    zh, core, zl, y = oj // 2, lax.rem(oj, 2), vert // 4, lax.rem(vert, 4)
    block = lax.rem(zh + y + 2 * zl, 4) * 2 + zl
    return x, oj, vert, core, jnp.bitwise_xor(block, vert), jnp.bitwise_xor(core, zl)


def load_pieces(pieces, chol, sems, first):
    pieces = list(pieces[:12]) + [beyond.at[at] for beyond in pieces[12:] for at in range(4)]
    copies = []
    for at, piece in enumerate(pieces):
        half = first if at // 2 % 2 == 0 else 1 - first
        target = chol.at[pl.ds(half * 4 + 2 * (at % 2), 2), at // 4]
        copies.append(pltpu.make_async_copy(piece, target, sems.at[at]))
    return copies


def pair_labels(occ, x, oj):
    pair = lax.broadcasted_iota(jnp.int32, (1, COLS), 1) // LO
    sym = jnp.zeros((1, COLS), jnp.int32)
    for row in range(8):
        for col in range(4):
            label = jnp.bitwise_xor(occ[x * 8 + row], occ[oj * 4 + col])
            sym = jnp.where(pair == row * 4 + col, label, sym)
    lo_row = lax.broadcasted_iota(jnp.int32, (LO, COLS), 0)
    lo_col = lax.broadcasted_iota(jnp.int32, (LO, COLS), 1) % LO
    return jnp.where(lo_row == lo_col, sym, -1)


def store_block(window, base, block, row):
    for hi in range(HI):
        at = row + hi * LO
        window[base : base + 2 * LO, hi * VB : (hi + 1) * VB] = jnp.concatenate(
            [block[at : at + LO, :VB], block[at : at + LO, VB:]], 0
        ).astype(jnp.bfloat16)


def spread_out(amp, spread):
    wide = amp.astype(jnp.float32).reshape(PAIRS, HI, LO, VB)
    for hi in range(HI):
        spread[:, hi * VB : (hi + 1) * VB] = wide[:, hi].reshape(COLS, VB).astype(jnp.bfloat16)


def collect(full, sym, ga, where, straight, turned):
    totals = {}
    for at, (gb, a, b) in enumerate(where):
        wanted = sym == jnp.bitwise_xor(ga, gb)
        slot = WB * a + b
        totals[slot] = jnp.where(wanted, full[at], totals.get(slot, 0.0))
        turned[gb, slot] = jnp.where(wanted, full[at], turned[gb, slot])
    for slot, total in totals.items():
        straight[ga, slot] = total


def finish(slots, straight, turned, own_ref, mirror_ref, x, core, vert):
    count = len(slots)
    actual = [lax.rem(x + hop, WB) for hop in HOPS]
    source = lax.broadcasted_iota(jnp.int32, (COLS, VB), 0) // LO
    lane = lax.broadcasted_iota(jnp.int32, (COLS, VB), 1) % PAIRS
    group = lax.broadcasted_iota(jnp.int32, (IRREPS, VB), 1) // PAIRS

    def summed(values):
        rows = [jnp.sum(values[:, WB * a + b], axis=1) for a, b in slots]
        return jnp.concatenate(rows, 0)

    def split(values, chosen, by_first):
        picked = exact_pick(values, chosen)
        lines = {}
        for at, (a, b) in enumerate(slots):
            line, wide = (a, b) if by_first else (b, a)
            part = jnp.where(group == actual[wide], picked[at * IRREPS : (at + 1) * IRREPS], 0.0)
            lines[line] = lines.get(line, 0.0) + part
        return lines

    own = split(summed(straight), (source == lane).astype(jnp.bfloat16), True)
    for line, value in own.items():
        for ga in range(IRREPS):
            there = (jnp.bitwise_xor(vert, ga), pl.ds(actual[line], 1))
            own_ref[there] = own_ref[there] + value[ga : ga + 1]
    every = summed(turned)
    target = core * 16 + (source % 4) * 4 + (source // 4) % 4
    for k in range(2):
        here = (source // 16) == jnp.bitwise_xor(core, k)
        other = split(every, ((lane == target) & here).astype(jnp.bfloat16), False)
        for line, value in other.items():
            for ga in range(IRREPS):
                there = (k, jnp.bitwise_xor(vert, ga), pl.ds(actual[line], 1))
                mirror_ref[there] = mirror_ref[there] + value[ga : ga + 1]


def amp_copy(amp_ref, amp, sems, flip, ga):
    return pltpu.make_async_copy(
        amp_ref.at[:, jnp.bitwise_xor(ga, flip)], amp.at[ga], sems.at[ga]
    )


def begin(occ_ref, amp_ref, pieces, chol, amp, occ, sems, flip, first):
    chol_sem, amp_sem, occ_sem = sems
    occ_copy = pltpu.make_async_copy(occ_ref, occ, occ_sem)
    occ_copy.start()
    amp_copy(amp_ref, amp, amp_sem, flip, 0).start()
    copies = load_pieces(pieces, chol, chol_sem, first)
    for copy in copies:
        copy.start()
    occ_copy.wait()
    for copy in copies:
        copy.wait()
    for ga in range(1, IRREPS):
        amp_copy(amp_ref, amp, amp_sem, flip, ga).start()


def early_kernel(occ_ref, amp_ref, *refs):
    pieces, (own_ref, mirror_ref) = refs[:12], refs[12:14]
    chol, amp, window, spread, straight, turned, occ, *sems = refs[14:]
    x, oj, vert, core, flip, first = place_of()
    begin(occ_ref, amp_ref, pieces, chol, amp, occ, sems, flip, first)
    sym = pair_labels(occ, x, oj)
    where = []
    for tile in range(12):
        for a in range(3):
            for at in (2 * tile, 2 * tile + 1):
                where.append((at // 3, a, at % 3))
    slots = [(a, b) for a in range(3) for b in range(3)]
    for a, b in slots:
        turned[:, WB * a + b] = jnp.zeros((IRREPS, LO, COLS), jnp.float32)
    own_ref[...] = jnp.zeros_like(own_ref)
    mirror_ref[...] = jnp.zeros_like(mirror_ref)

    def one_irrep(ga, carry):
        amp_copy(amp_ref, amp, sems[1], flip, ga).wait()
        spread_out(amp[ga], spread)
        left = chol[ga].reshape(3 * VB, PB)
        for tile in range(12):
            two = [chol[at // 3, at % 3] for at in (2 * tile, 2 * tile + 1)]
            block = lax.dot_general(
                left, jnp.concatenate(two, 0), NT, preferred_element_type=jnp.float32
            )
            for a in range(3):
                store_block(window, (tile * 3 + a) * 2 * LO, block, a * VB)
        full = []
        for start, stop in ((0, 32), (32, 72)):
            rows = window[start * LO : stop * LO]
            part = lax.dot_general(rows, spread[...], NT, preferred_element_type=jnp.float32)
            full.append(part.reshape(stop - start, LO, COLS))
        collect(jnp.concatenate(full, 0), sym, ga, where, straight, turned)
        return carry

    lax.fori_loop(0, IRREPS, one_irrep, 0)
    finish(slots, straight, turned, own_ref, mirror_ref, x, core, vert)


def late_kernel(occ_ref, amp_ref, own_in, mirror_in, *refs):
    pieces, (own_ref, mirror_ref) = refs[:13], refs[13:15]
    chol, amp, window, spread, straight, turned, occ, *sems = refs[15:]
    x, oj, vert, core, flip, first = place_of()
    begin(occ_ref, amp_ref, pieces, chol, amp, occ, sems, flip, first)
    sym = pair_labels(occ, x, oj)
    where = []
    for tile in range(4):
        for a in range(4):
            where += [(2 * tile, a, 3), (2 * tile + 1, a, 3)]
    for at in range(24):
        where.append((at // 3, 3, at % 3))
    slots = [(a, 3) for a in range(4)] + [(3, b) for b in range(3)]
    for a, b in slots:
        turned[:, WB * a + b] = jnp.zeros((IRREPS, LO, COLS), jnp.float32)
    own_ref[...] = own_in[...]
    mirror_ref[...] = mirror_in[...]

    def one_irrep(ga, carry):
        amp_copy(amp_ref, amp, sems[1], flip, ga).wait()
        spread_out(amp[ga], spread)
        left = chol[ga].reshape(WB * VB, PB)
        for tile in range(4):
            two = [chol[2 * tile, 3], chol[2 * tile + 1, 3]]
            block = lax.dot_general(
                left, jnp.concatenate(two, 0), NT, preferred_element_type=jnp.float32
            )
            for a in range(WB):
                store_block(window, (tile * WB + a) * 2 * LO, block, a * VB)
        for tile in range(12):
            two = [chol[at // 3, at % 3] for at in (2 * tile, 2 * tile + 1)]
            block = lax.dot_general(
                chol[ga, 3], jnp.concatenate(two, 0), NT, preferred_element_type=jnp.float32
            )
            store_block(window, (16 + tile) * 2 * LO, block, 0)
        for start, stop in ((0, 32), (32, 56)):
            rows = window[start * LO : stop * LO]
            part = lax.dot_general(rows, spread[...], NT, preferred_element_type=jnp.float32)
            part = part.reshape(stop - start, LO, COLS)
            collect(part, sym, ga, where[start:stop], straight, turned)
        return carry

    lax.fori_loop(0, IRREPS, one_irrep, 0)
    finish(slots, straight, turned, own_ref, mirror_ref, x, core, vert)


def ladder(kernel, slots, window, before, pieces):
    anywhere = pl.BlockSpec(memory_space=pl.ANY)
    whole = pl.BlockSpec(memory_space=pltpu.VMEM)
    occ, amp, *earlier = before
    return pl.pallas_call(
        kernel,
        out_shape=[
            jax.ShapeDtypeStruct((IRREPS, WB, VB), jnp.float32),
            jax.ShapeDtypeStruct((2, IRREPS, WB, VB), jnp.float32),
        ],
        in_specs=[anywhere] * 2 + [whole] * len(earlier) + [anywhere] * len(pieces),
        out_specs=[whole] * 2,
        scratch_shapes=[
            pltpu.VMEM((IRREPS, slots, VB, PB), jnp.bfloat16),
            pltpu.VMEM((IRREPS, PAIRS, VB, VB), jnp.bfloat16),
            pltpu.VMEM(window + (HI * VB,), jnp.bfloat16),
            pltpu.VMEM((COLS, HI * VB), jnp.bfloat16),
            pltpu.VMEM((IRREPS, WB * WB, LO, COLS), jnp.float32),
            pltpu.VMEM((IRREPS, WB * WB, LO, COLS), jnp.float32),
            pltpu.SMEM((PAIRS,), jnp.int32),
            pltpu.SemaphoreType.DMA((16,)),
            pltpu.SemaphoreType.DMA((8,)),
            pltpu.SemaphoreType.DMA,
        ],
        compiler_params=pltpu.CompilerParams(vmem_limit_bytes=50 * 2**20),
        cost_estimate=pl.CostEstimate(
            flops=8 * 10**9, bytes_accessed=12 * 10**6, transcendentals=0
        ),
    )(*before, *pieces)


def local(amplitudes, chol, occ_irrep):
    x = lax.axis_index("oi")
    core = lax.rem(lax.axis_index("oj"), 2)

    def permute(value, pairs):
        return lax.ppermute(value, AXES, pairs)

    mine = lax.dynamic_index_in_dim(chol[0], x, 1, False).T
    rows = [permute(mine, fetch_pairs(row)) for row in range(4)]
    near = [jnp.stack(rows[:2]), jnp.stack(rows[2:])]
    near[1], labels = lax.optimization_barrier((near[1], jnp.bitwise_and(occ_irrep, IRREPS - 1)))
    above = [permute(half, moved_pairs(lower)) for half in near]
    below = [permute(half, moved_pairs(upper)) for half in near]
    pieces = []
    for piece in (near, above, below):
        pieces += piece + [permute(half, moved_pairs(other_core)) for half in piece]
    beyond = jnp.where(core == 0, jnp.stack(pieces[4:8]), jnp.stack(pieces[8:12]))
    beyond = permute(beyond, moved_pairs(apart))
    occ_rows, occ_cols = amplitudes.shape[0], amplitudes.shape[1]
    amp = amplitudes.reshape(PAIRS, IRREPS, VB, VB)
    before = (labels, amp)
    mine, other = ladder(early_kernel, 3, (72 * LO,), before, pieces)
    before += (mine, other)
    pieces += [beyond]
    mine, other = ladder(late_kernel, 4, (56 * LO,), before, pieces)
    other = other[0] + permute(other[1], moved_pairs(other_core))
    total = mine + permute(other, moved_pairs(mirrored))
    total = jnp.sum(lax.all_to_all(total, "vert", 0, 0), axis=0)
    total = total.reshape(WB, WB, occ_rows, occ_cols)
    return jnp.transpose(total, (2, 3, 0, 1))[:, :, None]


def solution(mesh):
    return jax.shard_map(
        local,
        mesh=mesh,
        in_specs=(P("oi", "oj", None, None, None), P(("oj", "vert"), None, None, None), P()),
        out_specs=P("oi", "oj", "vert", None, None),
        check_vma=False,
    )
```

```python
import jax
import jax.numpy as jnp
from jax import lax
from jax.experimental import pallas as pl
from jax.experimental.pallas import tpu as pltpu
from jax.sharding import PartitionSpec as P

IRREPS = 8
VB = 128
PB = 256
WB = 4
LO = 8
HI = VB // LO
PAIRS = 32
HOPS = (0, 1, 3, 2)
COLS = PAIRS * LO
AXES = ("oi", "oj", "vert")
CHIPS = [
    (x, zh, core, zl, y)
    for x in range(4)
    for zh in range(4)
    for core in range(2)
    for zl in range(2)
    for y in range(4)
]
NT = (((1,), (1,)), ((), ()))


def flat_index(x, zh, core, zl, y):
    return x * 64 + (zh * 2 + core) * 8 + zl * 4 + y


def fetch_pairs(row):
    pairs = []
    for x, zh, core, zl, y in CHIPS:
        source = (x, (zh + y + 2 * zl) % 4, zl, core, y ^ row)
        pairs.append((flat_index(*source), flat_index(x, zh, core, zl, y)))
    return pairs


def moved_pairs(move):
    return [(flat_index(*d), flat_index(*move(*d))) for d in CHIPS]


def next_row(x, zh, core, zl, y):
    return (x, zh, core, zl, y ^ 1)


def lower(x, zh, core, zl, y):
    return ((x + 3) % 4, zh, core, zl, y)


def upper(x, zh, core, zl, y):
    return ((x + 1) % 4, zh, core, zl, y)


def apart(x, zh, core, zl, y):
    return ((x + (1 if core else 3)) % 4, zh, core, zl, y)


def other_core(x, zh, core, zl, y):
    return (x, zh, 1 - core, zl, y)


def mirrored(x, zh, core, zl, y):
    return (zh, x, core, zl, y)


def exact_pick(values, chosen):
    top = values.astype(jnp.bfloat16)
    rest = values - top.astype(jnp.float32)
    middle = rest.astype(jnp.bfloat16)
    low = (rest - middle.astype(jnp.float32)).astype(jnp.bfloat16)
    rows = values.shape[0]
    parts = jnp.dot(
        jnp.concatenate([top, middle, low], 0), chosen, preferred_element_type=jnp.float32
    )
    return parts[:rows] + (parts[rows : 2 * rows] + parts[2 * rows :])


def place_of():
    x, oj, vert = lax.axis_index("oi"), lax.axis_index("oj"), lax.axis_index("vert")
    zh, core, zl, y = oj // 2, lax.rem(oj, 2), vert // 4, lax.rem(vert, 4)
    block = lax.rem(zh + y + 2 * zl, 4) * 2 + zl
    return x, oj, vert, core, jnp.bitwise_xor(block, vert), jnp.bitwise_xor(core, zl)


def load_pieces(pieces, chol, sems, first):
    pieces = list(pieces[:12]) + [beyond.at[at] for beyond in pieces[12:] for at in range(4)]
    copies = []
    for at, piece in enumerate(pieces):
        half = first if at // 2 % 2 == 0 else 1 - first
        target = chol.at[pl.ds(half * 4 + 2 * (at % 2), 2), at // 4]
        copies.append(pltpu.make_async_copy(piece, target, sems.at[at]))
    return copies


def pair_labels(occ, x, oj):
    pair = lax.broadcasted_iota(jnp.int32, (1, COLS), 1) // LO
    sym = jnp.zeros((1, COLS), jnp.int32)
    for row in range(8):
        for col in range(4):
            label = jnp.bitwise_xor(occ[x * 8 + row], occ[oj * 4 + col])
            sym = jnp.where(pair == row * 4 + col, label, sym)
    lo_row = lax.broadcasted_iota(jnp.int32, (LO, COLS), 0)
    lo_col = lax.broadcasted_iota(jnp.int32, (LO, COLS), 1) % LO
    return jnp.where(lo_row == lo_col, sym, -1)


def store_block(window, base, block, row):
    for hi in range(HI):
        at = row + hi * LO
        window[base : base + 2 * LO, hi * VB : (hi + 1) * VB] = jnp.concatenate(
            [block[at : at + LO, :VB], block[at : at + LO, VB:]], 0
        ).astype(jnp.bfloat16)


def spread_out(amp, spread):
    wide = amp.astype(jnp.float32).reshape(PAIRS, HI, LO, VB)
    for hi in range(HI):
        spread[:, hi * VB : (hi + 1) * VB] = wide[:, hi].reshape(COLS, VB).astype(jnp.bfloat16)


def collect(full, sym, ga, where, straight, turned):
    totals = {}
    for at, (gb, a, b) in enumerate(where):
        wanted = sym == jnp.bitwise_xor(ga, gb)
        slot = WB * a + b
        totals[slot] = jnp.where(wanted, full[at], totals.get(slot, 0.0))
        turned[gb, slot] = jnp.where(wanted, full[at], turned[gb, slot])
    for slot, total in totals.items():
        straight[ga, slot] = total


def finish(slots, straight, turned, own_ref, mirror_ref, x, core, vert):
    count = len(slots)
    actual = [lax.rem(x + hop, WB) for hop in HOPS]
    source = lax.broadcasted_iota(jnp.int32, (COLS, VB), 0) // LO
    lane = lax.broadcasted_iota(jnp.int32, (COLS, VB), 1) % PAIRS
    group = lax.broadcasted_iota(jnp.int32, (IRREPS, VB), 1) // PAIRS

    def summed(values):
        rows = [jnp.sum(values[:, WB * a + b], axis=1) for a, b in slots]
        return jnp.concatenate(rows, 0)

    def split(values, chosen, by_first):
        picked = exact_pick(values, chosen)
        lines = {}
        for at, (a, b) in enumerate(slots):
            line, wide = (a, b) if by_first else (b, a)
            part = jnp.where(group == actual[wide], picked[at * IRREPS : (at + 1) * IRREPS], 0.0)
            lines[line] = lines.get(line, 0.0) + part
        return lines

    own = split(summed(straight), (source == lane).astype(jnp.bfloat16), True)
    for line, value in own.items():
        for ga in range(IRREPS):
            there = (jnp.bitwise_xor(vert, ga), pl.ds(actual[line], 1))
            own_ref[there] = own_ref[there] + value[ga : ga + 1]
    every = summed(turned)
    target = core * 16 + (source % 4) * 4 + (source // 4) % 4
    for k in range(2):
        here = (source // 16) == jnp.bitwise_xor(core, k)
        other = split(every, ((lane == target) & here).astype(jnp.bfloat16), False)
        for line, value in other.items():
            for ga in range(IRREPS):
                there = (k, jnp.bitwise_xor(vert, ga), pl.ds(actual[line], 1))
                mirror_ref[there] = mirror_ref[there] + value[ga : ga + 1]


def amp_copy(amp_ref, amp, sems, flip, ga):
    return pltpu.make_async_copy(
        amp_ref.at[:, jnp.bitwise_xor(ga, flip)], amp.at[ga], sems.at[ga]
    )


def begin(occ_ref, amp_ref, pieces, chol, amp, occ, sems, flip, first, x, oj, slots, turned):
    chol_sem, amp_sem, occ_sem = sems
    occ_copy = pltpu.make_async_copy(occ_ref, occ, occ_sem)
    occ_copy.start()
    amp_copy(amp_ref, amp, amp_sem, flip, 0).start()
    copies = load_pieces(pieces, chol, chol_sem, first)
    for copy in copies:
        copy.start()
    occ_copy.wait()
    sym = pair_labels(occ, x, oj)
    for a, b in slots:
        turned[:, WB * a + b] = jnp.zeros((IRREPS, LO, COLS), jnp.float32)
    for copy in copies:
        copy.wait()
    for ga in range(1, IRREPS):
        amp_copy(amp_ref, amp, amp_sem, flip, ga).start()
    return sym


def early_kernel(occ_ref, amp_ref, *refs):
    pieces, (own_ref, mirror_ref) = refs[:12], refs[12:14]
    chol, amp, window, spread, straight, turned, occ, *sems = refs[14:]
    x, oj, vert, core, flip, first = place_of()
    where = []
    for tile in range(12):
        for a in range(3):
            for at in (2 * tile, 2 * tile + 1):
                where.append((at // 3, a, at % 3))
    slots = [(a, b) for a in range(3) for b in range(3)]
    sym = begin(
        occ_ref, amp_ref, pieces, chol, amp, occ, sems, flip, first, x, oj, slots, turned
    )
    own_ref[...] = jnp.zeros_like(own_ref)
    mirror_ref[...] = jnp.zeros_like(mirror_ref)

    def one_irrep(ga, carry):
        amp_copy(amp_ref, amp, sems[1], flip, ga).wait()
        spread_out(amp[ga], spread)
        left = chol[ga].reshape(3 * VB, PB)
        for tile in range(12):
            two = [chol[at // 3, at % 3] for at in (2 * tile, 2 * tile + 1)]
            block = lax.dot_general(
                left, jnp.concatenate(two, 0), NT, preferred_element_type=jnp.float32
            )
            for a in range(3):
                store_block(window, (tile * 3 + a) * 2 * LO, block, a * VB)
        full = []
        for start, stop in ((0, 32), (32, 72)):
            rows = window[start * LO : stop * LO]
            part = lax.dot_general(rows, spread[...], NT, preferred_element_type=jnp.float32)
            full.append(part.reshape(stop - start, LO, COLS))
        collect(jnp.concatenate(full, 0), sym, ga, where, straight, turned)
        return carry

    lax.fori_loop(0, IRREPS, one_irrep, 0)
    finish(slots, straight, turned, own_ref, mirror_ref, x, core, vert)


def late_kernel(occ_ref, amp_ref, own_in, mirror_in, *refs):
    pieces, (own_ref, mirror_ref) = refs[:13], refs[13:15]
    chol, amp, window, spread, straight, turned, occ, *sems = refs[15:]
    x, oj, vert, core, flip, first = place_of()
    where = []
    for tile in range(4):
        for a in range(4):
            where += [(2 * tile, a, 3), (2 * tile + 1, a, 3)]
    for at in range(24):
        where.append((at // 3, 3, at % 3))
    slots = [(a, 3) for a in range(4)] + [(3, b) for b in range(3)]
    sym = begin(
        occ_ref, amp_ref, pieces, chol, amp, occ, sems, flip, first, x, oj, slots, turned
    )
    own_ref[...] = own_in[...]
    mirror_ref[...] = mirror_in[...]

    def two_irreps(step, carry):
        last = chol[pl.ds(2 * step, 2), 3].reshape(2 * VB, PB)
        for tile in range(12):
            two = [chol[at // 3, at % 3] for at in (2 * tile, 2 * tile + 1)]
            block = lax.dot_general(
                last, jnp.concatenate(two, 0), NT, preferred_element_type=jnp.float32
            )
            for u in range(2):
                store_block(window, (32 + 24 * u + 2 * tile) * LO, block, u * VB)

        def one_irrep(u, carry):
            ga = 2 * step + u
            amp_copy(amp_ref, amp, sems[1], flip, ga).wait()
            spread_out(amp[ga], spread)
            left = chol[ga].reshape(WB * VB, PB)
            for tile in range(4):
                two = [chol[2 * tile, 3], chol[2 * tile + 1, 3]]
                block = lax.dot_general(
                    left, jnp.concatenate(two, 0), NT, preferred_element_type=jnp.float32
                )
                for a in range(WB):
                    store_block(window, (tile * WB + a) * 2 * LO, block, a * VB)
            lower = window[pl.ds(pl.multiple_of((32 + 24 * u) * LO, 2 * LO), 24 * LO)]
            for rows, start, stop in ((window[: 32 * LO], 0, 32), (lower, 32, 56)):
                part = lax.dot_general(rows, spread[...], NT, preferred_element_type=jnp.float32)
                part = part.reshape(stop - start, LO, COLS)
                collect(part, sym, ga, where[start:stop], straight, turned)
            return carry

        return lax.fori_loop(0, 2, one_irrep, carry)

    lax.fori_loop(0, IRREPS // 2, two_irreps, 0)
    finish(slots, straight, turned, own_ref, mirror_ref, x, core, vert)


def ladder(kernel, slots, window, before, pieces):
    anywhere = pl.BlockSpec(memory_space=pl.ANY)
    whole = pl.BlockSpec(memory_space=pltpu.VMEM)
    occ, amp, *earlier = before
    return pl.pallas_call(
        kernel,
        out_shape=[
            jax.ShapeDtypeStruct((IRREPS, WB, VB), jnp.float32),
            jax.ShapeDtypeStruct((2, IRREPS, WB, VB), jnp.float32),
        ],
        in_specs=[anywhere] * 2 + [whole] * len(earlier) + [anywhere] * len(pieces),
        out_specs=[whole] * 2,
        scratch_shapes=[
            pltpu.VMEM((IRREPS, slots, VB, PB), jnp.bfloat16),
            pltpu.VMEM((IRREPS, PAIRS, VB, VB), jnp.bfloat16),
            pltpu.VMEM(window + (HI * VB,), jnp.bfloat16),
            pltpu.VMEM((COLS, HI * VB), jnp.bfloat16),
            pltpu.VMEM((IRREPS, WB * WB, LO, COLS), jnp.float32),
            pltpu.VMEM((IRREPS, WB * WB, LO, COLS), jnp.float32),
            pltpu.SMEM((PAIRS,), jnp.int32),
            pltpu.SemaphoreType.DMA((16,)),
            pltpu.SemaphoreType.DMA((8,)),
            pltpu.SemaphoreType.DMA,
        ],
        compiler_params=pltpu.CompilerParams(vmem_limit_bytes=50 * 2**20),
        cost_estimate=pl.CostEstimate(
            flops=8 * 10**9, bytes_accessed=12 * 10**6, transcendentals=0
        ),
    )(*before, *pieces)


def local(amplitudes, chol, occ_irrep):
    x = lax.axis_index("oi")
    core = lax.rem(lax.axis_index("oj"), 2)

    def permute(value, pairs):
        return lax.ppermute(value, AXES, pairs)

    mine = lax.dynamic_index_in_dim(chol[0], x, 1, False).T
    pair = jnp.stack([mine, permute(mine, moved_pairs(next_row))])
    near = [permute(pair, fetch_pairs(row)) for row in (0, 2)]
    near[1], labels = lax.optimization_barrier((near[1], jnp.bitwise_and(occ_irrep, IRREPS - 1)))
    above = [permute(half, moved_pairs(lower)) for half in near]
    below = [permute(half, moved_pairs(upper)) for half in near]
    swap = moved_pairs(other_core)
    beside = [permute(jnp.stack([above[far], below[far]]), swap) for far in range(2)]
    pieces = near + [permute(half, swap) for half in near]
    pieces += above + [beside[0][0], beside[1][0]] + below + [beside[0][1], beside[1][1]]
    beyond = jnp.where(core == 0, jnp.stack(pieces[4:8]), jnp.stack(pieces[8:12]))
    beyond = permute(beyond, moved_pairs(apart))
    occ_rows, occ_cols = amplitudes.shape[0], amplitudes.shape[1]
    amp = amplitudes.reshape(PAIRS, IRREPS, VB, VB)
    before = (labels, amp)
    mine, other = ladder(early_kernel, 3, (72 * LO,), before, pieces)
    before += (mine, other)
    pieces += [beyond]
    mine, other = ladder(late_kernel, 4, (80 * LO,), before, pieces)
    other = other[0] + permute(other[1], moved_pairs(other_core))
    total = mine + permute(other, moved_pairs(mirrored))
    total = jnp.sum(lax.all_to_all(total, "vert", 0, 0), axis=0)
    total = total.reshape(WB, WB, occ_rows, occ_cols)
    return jnp.transpose(total, (2, 3, 0, 1))[:, :, None]


def solution(mesh):
    return jax.shard_map(
        local,
        mesh=mesh,
        in_specs=(P("oi", "oj", None, None, None), P(("oj", "vert"), None, None, None), P()),
        out_specs=P("oi", "oj", "vert", None, None),
        check_vma=False,
    )
```

```python
import jax
import jax.numpy as jnp
from jax import lax
from jax.experimental import pallas as pl
from jax.experimental.pallas import tpu as pltpu
from jax.sharding import PartitionSpec as P

IRREPS = 8
VB = 128
PB = 256
WB = 4
LO = 8
HI = VB // LO
PAIRS = 32
HOPS = (0, 1, 3, 2)
COLS = PAIRS * LO
AXES = ("oi", "oj", "vert")
CHIPS = [
    (x, zh, core, zl, y)
    for x in range(4)
    for zh in range(4)
    for core in range(2)
    for zl in range(2)
    for y in range(4)
]
NT = (((1,), (1,)), ((), ()))


def flat_index(x, zh, core, zl, y):
    return x * 64 + (zh * 2 + core) * 8 + zl * 4 + y


def fetch_pairs(row):
    pairs = []
    for x, zh, core, zl, y in CHIPS:
        source = (x, (zh + y + 2 * zl) % 4, zl, core, y ^ row)
        pairs.append((flat_index(*source), flat_index(x, zh, core, zl, y)))
    return pairs


def moved_pairs(move):
    return [(flat_index(*d), flat_index(*move(*d))) for d in CHIPS]


def next_row(x, zh, core, zl, y):
    return (x, zh, core, zl, y ^ 1)


def lower(x, zh, core, zl, y):
    return ((x + 3) % 4, zh, core, zl, y)


def upper(x, zh, core, zl, y):
    return ((x + 1) % 4, zh, core, zl, y)


def apart(x, zh, core, zl, y):
    return ((x + (1 if core else 3)) % 4, zh, core, zl, y)


def other_core(x, zh, core, zl, y):
    return (x, zh, 1 - core, zl, y)


def mirrored(x, zh, core, zl, y):
    return (zh, x, core, zl, y)


def exact_pick(values, chosen):
    top = values.astype(jnp.bfloat16)
    rest = values - top.astype(jnp.float32)
    middle = rest.astype(jnp.bfloat16)
    low = (rest - middle.astype(jnp.float32)).astype(jnp.bfloat16)
    rows = values.shape[0]
    parts = jnp.dot(
        jnp.concatenate([top, middle, low], 0), chosen, preferred_element_type=jnp.float32
    )
    return parts[:rows] + (parts[rows : 2 * rows] + parts[2 * rows :])


def place_of():
    x, oj, vert = lax.axis_index("oi"), lax.axis_index("oj"), lax.axis_index("vert")
    zh, core, zl, y = oj // 2, lax.rem(oj, 2), vert // 4, lax.rem(vert, 4)
    block = lax.rem(zh + y + 2 * zl, 4) * 2 + zl
    return x, oj, vert, core, jnp.bitwise_xor(block, vert), jnp.bitwise_xor(core, zl)


def load_pieces(pieces, chol, sems, first):
    pieces = list(pieces[:12]) + [beyond.at[at] for beyond in pieces[12:] for at in range(4)]
    copies = []
    for at, piece in enumerate(pieces):
        half = first if at // 2 % 2 == 0 else 1 - first
        target = chol.at[pl.ds(half * 4 + 2 * (at % 2), 2), at // 4]
        copies.append(pltpu.make_async_copy(piece, target, sems.at[at]))
    return copies


def pair_labels(occ, x, oj):
    pair = lax.broadcasted_iota(jnp.int32, (1, COLS), 1) // LO
    sym = jnp.zeros((1, COLS), jnp.int32)
    for row in range(8):
        for col in range(4):
            label = jnp.bitwise_xor(occ[x * 8 + row], occ[oj * 4 + col])
            sym = jnp.where(pair == row * 4 + col, label, sym)
    lo_row = lax.broadcasted_iota(jnp.int32, (LO, COLS), 0)
    lo_col = lax.broadcasted_iota(jnp.int32, (LO, COLS), 1) % LO
    return jnp.where(lo_row == lo_col, sym, -1)


def store_block(window, base, block, row):
    for hi in range(HI):
        at = row + hi * LO
        window[base : base + 2 * LO, hi * VB : (hi + 1) * VB] = jnp.concatenate(
            [block[at : at + LO, :VB], block[at : at + LO, VB:]], 0
        ).astype(jnp.bfloat16)


def spread_out(amp, spread):
    wide = amp.astype(jnp.float32).reshape(PAIRS, HI, LO, VB)
    for hi in range(HI):
        spread[:, hi * VB : (hi + 1) * VB] = wide[:, hi].reshape(COLS, VB).astype(jnp.bfloat16)


def collect(full, sym, ga, where, straight, turned):
    totals = {}
    for at, (gb, a, b) in enumerate(where):
        wanted = sym == jnp.bitwise_xor(ga, gb)
        slot = WB * a + b
        totals[slot] = jnp.where(wanted, full[at], totals.get(slot, 0.0))
        turned[gb, slot] = jnp.where(wanted, full[at], turned[gb, slot])
    for slot, total in totals.items():
        straight[ga, slot] = total


def finish(slots, straight, turned, own_ref, mirror_ref, x, core, vert):
    count = len(slots)
    actual = [lax.rem(x + hop, WB) for hop in HOPS]
    source = lax.broadcasted_iota(jnp.int32, (COLS, VB), 0) // LO
    lane = lax.broadcasted_iota(jnp.int32, (COLS, VB), 1) % PAIRS
    group = lax.broadcasted_iota(jnp.int32, (IRREPS, VB), 1) // PAIRS

    def summed(values):
        rows = [jnp.sum(values[:, WB * a + b], axis=1) for a, b in slots]
        return jnp.concatenate(rows, 0)

    def split(values, chosen, by_first):
        picked = exact_pick(values, chosen)
        lines = {}
        for at, (a, b) in enumerate(slots):
            line, wide = (a, b) if by_first else (b, a)
            part = jnp.where(group == actual[wide], picked[at * IRREPS : (at + 1) * IRREPS], 0.0)
            lines[line] = lines.get(line, 0.0) + part
        return lines

    own = split(summed(straight), (source == lane).astype(jnp.bfloat16), True)
    for line, value in own.items():
        for ga in range(IRREPS):
            there = (jnp.bitwise_xor(vert, ga), pl.ds(actual[line], 1))
            own_ref[there] = own_ref[there] + value[ga : ga + 1]
    every = summed(turned)
    target = core * 16 + (source % 4) * 4 + (source // 4) % 4
    for k in range(2):
        here = (source // 16) == jnp.bitwise_xor(core, k)
        other = split(every, ((lane == target) & here).astype(jnp.bfloat16), False)
        for line, value in other.items():
            for ga in range(IRREPS):
                there = (k, jnp.bitwise_xor(vert, ga), pl.ds(actual[line], 1))
                mirror_ref[there] = mirror_ref[there] + value[ga : ga + 1]


def amp_copy(amp_ref, amp, sems, flip, ga):
    return pltpu.make_async_copy(
        amp_ref.at[:, jnp.bitwise_xor(ga, flip)], amp.at[ga], sems.at[ga]
    )


def begin(occ_ref, amp_ref, pieces, chol, amp, occ, sems, flip, first, x, oj, slots, turned):
    chol_sem, amp_sem, occ_sem = sems
    occ_copy = pltpu.make_async_copy(occ_ref, occ, occ_sem)
    occ_copy.start()
    amp_copy(amp_ref, amp, amp_sem, flip, 0).start()
    copies = load_pieces(pieces, chol, chol_sem, first)
    for copy in copies:
        copy.start()
    occ_copy.wait()
    sym = pair_labels(occ, x, oj)
    for a, b in slots:
        turned[:, WB * a + b] = jnp.zeros((IRREPS, LO, COLS), jnp.float32)
    for copy in copies:
        copy.wait()
    for ga in range(1, IRREPS):
        amp_copy(amp_ref, amp, amp_sem, flip, ga).start()
    return sym


def early_kernel(occ_ref, amp_ref, *refs):
    pieces, (own_ref, mirror_ref) = refs[:12], refs[12:14]
    chol, amp, window, spread, straight, turned, occ, *sems = refs[14:]
    x, oj, vert, core, flip, first = place_of()
    where = []
    for tile in range(12):
        for a in range(3):
            for at in (2 * tile, 2 * tile + 1):
                where.append((at // 3, a, at % 3))
    slots = [(a, b) for a in range(3) for b in range(3)]
    sym = begin(
        occ_ref, amp_ref, pieces, chol, amp, occ, sems, flip, first, x, oj, slots, turned
    )
    own_ref[...] = jnp.zeros_like(own_ref)
    mirror_ref[...] = jnp.zeros_like(mirror_ref)

    def one_irrep(ga, carry):
        amp_copy(amp_ref, amp, sems[1], flip, ga).wait()
        spread_out(amp[ga], spread)
        left = chol[ga].reshape(3 * VB, PB)
        for tile in range(12):
            two = [chol[at // 3, at % 3] for at in (2 * tile, 2 * tile + 1)]
            block = lax.dot_general(
                left, jnp.concatenate(two, 0), NT, preferred_element_type=jnp.float32
            )
            for a in range(3):
                store_block(window, (tile * 3 + a) * 2 * LO, block, a * VB)
        full = []
        for start, stop in ((0, 32), (32, 72)):
            rows = window[start * LO : stop * LO]
            part = lax.dot_general(rows, spread[...], NT, preferred_element_type=jnp.float32)
            full.append(part.reshape(stop - start, LO, COLS))
        collect(jnp.concatenate(full, 0), sym, ga, where, straight, turned)
        return carry

    lax.fori_loop(0, IRREPS, one_irrep, 0)
    finish(slots, straight, turned, own_ref, mirror_ref, x, core, vert)


def late_kernel(occ_ref, amp_ref, own_in, mirror_in, *refs):
    pieces, (own_ref, mirror_ref) = refs[:13], refs[13:15]
    chol, amp, window, spread, straight, turned, occ, *sems = refs[15:]
    x, oj, vert, core, flip, first = place_of()
    where = []
    for tile in range(4):
        for a in range(4):
            where += [(2 * tile, a, 3), (2 * tile + 1, a, 3)]
    for at in range(24):
        where.append((at // 3, 3, at % 3))
    slots = [(a, 3) for a in range(4)] + [(3, b) for b in range(3)]
    sym = begin(
        occ_ref, amp_ref, pieces, chol, amp, occ, sems, flip, first, x, oj, slots, turned
    )
    own_ref[...] = own_in[...]
    mirror_ref[...] = mirror_in[...]

    def two_irreps(step, carry):
        last = chol[pl.ds(2 * step, 2), 3].reshape(2 * VB, PB)
        for tile in range(12):
            two = [chol[at // 3, at % 3] for at in (2 * tile, 2 * tile + 1)]
            block = lax.dot_general(
                last, jnp.concatenate(two, 0), NT, preferred_element_type=jnp.float32
            )
            for u in range(2):
                store_block(window, (32 + 24 * u + 2 * tile) * LO, block, u * VB)

        def one_irrep(u, carry):
            ga = 2 * step + u
            amp_copy(amp_ref, amp, sems[1], flip, ga).wait()
            spread_out(amp[ga], spread)
            left = chol[ga].reshape(WB * VB, PB)
            for tile in range(4):
                two = [chol[2 * tile, 3], chol[2 * tile + 1, 3]]
                block = lax.dot_general(
                    left, jnp.concatenate(two, 0), NT, preferred_element_type=jnp.float32
                )
                for a in range(WB):
                    store_block(window, (tile * WB + a) * 2 * LO, block, a * VB)
            lower = window[pl.ds(pl.multiple_of((32 + 24 * u) * LO, 2 * LO), 24 * LO)]
            for rows, start, stop in ((window[: 32 * LO], 0, 32), (lower, 32, 56)):
                part = lax.dot_general(rows, spread[...], NT, preferred_element_type=jnp.float32)
                part = part.reshape(stop - start, LO, COLS)
                collect(part, sym, ga, where[start:stop], straight, turned)
            return carry

        return lax.fori_loop(0, 2, one_irrep, carry)

    lax.fori_loop(0, IRREPS // 2, two_irreps, 0)
    finish(slots, straight, turned, own_ref, mirror_ref, x, core, vert)


def ladder(kernel, slots, window, before, pieces):
    anywhere = pl.BlockSpec(memory_space=pl.ANY)
    whole = pl.BlockSpec(memory_space=pltpu.VMEM)
    occ, amp, *earlier = before
    return pl.pallas_call(
        kernel,
        out_shape=[
            jax.ShapeDtypeStruct((IRREPS, WB, VB), jnp.float32),
            jax.ShapeDtypeStruct((2, IRREPS, WB, VB), jnp.float32),
        ],
        in_specs=[anywhere] * 2 + [whole] * len(earlier) + [anywhere] * len(pieces),
        out_specs=[whole] * 2,
        scratch_shapes=[
            pltpu.VMEM((IRREPS, slots, VB, PB), jnp.bfloat16),
            pltpu.VMEM((IRREPS, PAIRS, VB, VB), jnp.bfloat16),
            pltpu.VMEM(window + (HI * VB,), jnp.bfloat16),
            pltpu.VMEM((COLS, HI * VB), jnp.bfloat16),
            pltpu.VMEM((IRREPS, WB * WB, LO, COLS), jnp.float32),
            pltpu.VMEM((IRREPS, WB * WB, LO, COLS), jnp.float32),
            pltpu.SMEM((PAIRS,), jnp.int32),
            pltpu.SemaphoreType.DMA((16,)),
            pltpu.SemaphoreType.DMA((8,)),
            pltpu.SemaphoreType.DMA,
        ],
        compiler_params=pltpu.CompilerParams(vmem_limit_bytes=50 * 2**20),
        cost_estimate=pl.CostEstimate(
            flops=8 * 10**9, bytes_accessed=12 * 10**6, transcendentals=0
        ),
    )(*before, *pieces)


def local(amplitudes, chol, occ_irrep):
    x = lax.axis_index("oi")
    core = lax.rem(lax.axis_index("oj"), 2)

    def permute(value, pairs):
        return lax.ppermute(value, AXES, pairs)

    mine = lax.dynamic_index_in_dim(chol[0], x, 1, False).T
    pair = jnp.stack([mine, permute(mine, moved_pairs(next_row))])
    near = [permute(pair, fetch_pairs(row)) for row in (0, 2)]
    near[1], labels = lax.optimization_barrier((near[1], jnp.bitwise_and(occ_irrep, IRREPS - 1)))
    above = [permute(half, moved_pairs(lower)) for half in near]
    below = [permute(half, moved_pairs(upper)) for half in near]
    swap = moved_pairs(other_core)
    beside = [permute(jnp.stack([above[far], below[far]]), swap) for far in range(2)]
    pieces = near + [permute(half, swap) for half in near]
    pieces += above + [beside[0][0], beside[1][0]] + below + [beside[0][1], beside[1][1]]
    beyond = jnp.where(core == 0, jnp.stack(pieces[4:8]), jnp.stack(pieces[8:12]))
    beyond = permute(beyond, moved_pairs(apart))
    occ_rows, occ_cols = amplitudes.shape[0], amplitudes.shape[1]
    amp = amplitudes.reshape(PAIRS, IRREPS, VB, VB)
    before = (labels, amp)
    mine, other = ladder(early_kernel, 3, (72 * LO,), before, pieces)
    before += (mine, other)
    pieces += [beyond]
    mine, other = ladder(late_kernel, 4, (80 * LO,), before, pieces)
    every = jnp.concatenate([mine, other[0], other[1]], axis=1)
    every = jnp.sum(lax.all_to_all(every, "vert", 0, 0), axis=0)
    other = every[WB : 2 * WB] + permute(every[2 * WB :], moved_pairs(other_core))
    total = every[:WB] + permute(other, moved_pairs(mirrored))
    total = total.reshape(WB, WB, occ_rows, occ_cols)
    return jnp.transpose(total, (2, 3, 0, 1))[:, :, None]


def solution(mesh):
    return jax.shard_map(
        local,
        mesh=mesh,
        in_specs=(P("oi", "oj", None, None, None), P(("oj", "vert"), None, None, None), P()),
        out_specs=P("oi", "oj", "vert", None, None),
        check_vma=False,
    )
```

```python
import jax
import jax.numpy as jnp
from jax import lax
from jax.experimental import pallas as pl
from jax.experimental.pallas import tpu as pltpu
from jax.sharding import PartitionSpec as P

IRREPS = 8
VB = 128
PB = 256
WB = 4
LO = 8
HI = VB // LO
PAIRS = 32
HOPS = (0, 1, 3, 2)
COLS = PAIRS * LO
AXES = ("oi", "oj", "vert")
CHIPS = [
    (x, zh, core, zl, y)
    for x in range(4)
    for zh in range(4)
    for core in range(2)
    for zl in range(2)
    for y in range(4)
]
NT = (((1,), (1,)), ((), ()))


def flat_index(x, zh, core, zl, y):
    return x * 64 + (zh * 2 + core) * 8 + zl * 4 + y


def fetch_pairs(row):
    pairs = []
    for x, zh, core, zl, y in CHIPS:
        source = (x, (zh + y + 2 * zl) % 4, zl, core, y ^ row)
        pairs.append((flat_index(*source), flat_index(x, zh, core, zl, y)))
    return pairs


def moved_pairs(move):
    return [(flat_index(*d), flat_index(*move(*d))) for d in CHIPS]


def next_row(x, zh, core, zl, y):
    return (x, zh, core, zl, y ^ 1)


def lower(x, zh, core, zl, y):
    return ((x + 3) % 4, zh, core, zl, y)


def upper(x, zh, core, zl, y):
    return ((x + 1) % 4, zh, core, zl, y)


def apart(x, zh, core, zl, y):
    return ((x + (1 if core else 3)) % 4, zh, core, zl, y)


def other_core(x, zh, core, zl, y):
    return (x, zh, 1 - core, zl, y)


def mirrored(x, zh, core, zl, y):
    return (zh, x, core, zl, y)


def exact_pick(values, chosen):
    top = values.astype(jnp.bfloat16)
    rest = values - top.astype(jnp.float32)
    middle = rest.astype(jnp.bfloat16)
    low = (rest - middle.astype(jnp.float32)).astype(jnp.bfloat16)
    rows = values.shape[0]
    parts = jnp.dot(
        jnp.concatenate([top, middle, low], 0), chosen, preferred_element_type=jnp.float32
    )
    return parts[:rows] + (parts[rows : 2 * rows] + parts[2 * rows :])


def place_of():
    x, oj, vert = lax.axis_index("oi"), lax.axis_index("oj"), lax.axis_index("vert")
    zh, core, zl, y = oj // 2, lax.rem(oj, 2), vert // 4, lax.rem(vert, 4)
    block = lax.rem(zh + y + 2 * zl, 4) * 2 + zl
    return x, oj, vert, core, jnp.bitwise_xor(block, vert), jnp.bitwise_xor(core, zl)


def load_pieces(pieces, chol, sems, first):
    pieces = list(pieces[:12]) + [beyond.at[at] for beyond in pieces[12:] for at in range(4)]
    copies = []
    for at, piece in enumerate(pieces):
        half = first if at // 2 % 2 == 0 else 1 - first
        target = chol.at[pl.ds(half * 4 + 2 * (at % 2), 2), at // 4]
        copies.append(pltpu.make_async_copy(piece, target, sems.at[at]))
    return copies


def pair_labels(occ, x, oj):
    pair = lax.broadcasted_iota(jnp.int32, (1, COLS), 1) // LO
    sym = jnp.zeros((1, COLS), jnp.int32)
    for row in range(8):
        for col in range(4):
            label = jnp.bitwise_xor(occ[x * 8 + row], occ[oj * 4 + col])
            sym = jnp.where(pair == row * 4 + col, label, sym)
    lo_row = lax.broadcasted_iota(jnp.int32, (LO, COLS), 0)
    lo_col = lax.broadcasted_iota(jnp.int32, (LO, COLS), 1) % LO
    return jnp.where(lo_row == lo_col, sym, -1)


def store_block(window, base, block, row):
    for hi in range(HI):
        at = row + hi * LO
        window[base : base + 2 * LO, hi * VB : (hi + 1) * VB] = jnp.concatenate(
            [block[at : at + LO, :VB], block[at : at + LO, VB:]], 0
        ).astype(jnp.bfloat16)


def spread_out(amp, spread):
    wide = amp.astype(jnp.float32).reshape(PAIRS, HI, LO, VB)
    for hi in range(HI):
        spread[:, hi * VB : (hi + 1) * VB] = wide[:, hi].reshape(COLS, VB).astype(jnp.bfloat16)


def collect(full, sym, ga, where, straight, turned):
    totals = {}
    for at, (gb, a, b) in enumerate(where):
        wanted = sym == jnp.bitwise_xor(ga, gb)
        slot = WB * a + b
        totals[slot] = jnp.where(wanted, full[at], totals.get(slot, 0.0))
        turned[gb, slot] = jnp.where(wanted, full[at], turned[gb, slot])
    for slot, total in totals.items():
        straight[ga, slot] = total


def finish(slots, straight, turned, own_ref, mirror_ref, x, core, vert):
    count = len(slots)
    actual = [lax.rem(x + hop, WB) for hop in HOPS]
    source = lax.broadcasted_iota(jnp.int32, (COLS, VB), 0) // LO
    lane = lax.broadcasted_iota(jnp.int32, (COLS, VB), 1) % PAIRS
    group = lax.broadcasted_iota(jnp.int32, (IRREPS, VB), 1) // PAIRS

    def summed(values):
        rows = [jnp.sum(values[:, WB * a + b], axis=1) for a, b in slots]
        return jnp.concatenate(rows, 0)

    def split(values, chosen, by_first):
        picked = exact_pick(values, chosen)
        lines = {}
        for at, (a, b) in enumerate(slots):
            line, wide = (a, b) if by_first else (b, a)
            part = jnp.where(group == actual[wide], picked[at * IRREPS : (at + 1) * IRREPS], 0.0)
            lines[line] = lines.get(line, 0.0) + part
        return lines

    own = split(summed(straight), (source == lane).astype(jnp.bfloat16), True)
    for line, value in own.items():
        for ga in range(IRREPS):
            there = (jnp.bitwise_xor(vert, ga), pl.ds(actual[line], 1))
            own_ref[there] = own_ref[there] + value[ga : ga + 1]
    every = summed(turned)
    target = (source // 16) * 16 + (source % 4) * 4 + (source // 4) % 4
    other = split(every, (lane == target).astype(jnp.bfloat16), False)
    for line, value in other.items():
        for ga in range(IRREPS):
            there = (jnp.bitwise_xor(vert, ga), pl.ds(actual[line], 1))
            mirror_ref[there] = mirror_ref[there] + value[ga : ga + 1]


def amp_copy(amp_ref, amp, sems, flip, ga):
    return pltpu.make_async_copy(
        amp_ref.at[:, jnp.bitwise_xor(ga, flip)], amp.at[ga], sems.at[ga]
    )


def begin(occ_ref, amp_ref, pieces, chol, amp, occ, sems, flip, first, x, oj, slots, turned):
    chol_sem, amp_sem, occ_sem = sems
    occ_copy = pltpu.make_async_copy(occ_ref, occ, occ_sem)
    occ_copy.start()
    amp_copy(amp_ref, amp, amp_sem, flip, 0).start()
    copies = load_pieces(pieces, chol, chol_sem, first)
    for copy in copies:
        copy.start()
    occ_copy.wait()
    sym = pair_labels(occ, x, oj)
    for a, b in slots:
        turned[:, WB * a + b] = jnp.zeros((IRREPS, LO, COLS), jnp.float32)
    for copy in copies:
        copy.wait()
    for ga in range(1, IRREPS):
        amp_copy(amp_ref, amp, amp_sem, flip, ga).start()
    return sym


def early_kernel(occ_ref, amp_ref, *refs):
    pieces, (own_ref, mirror_ref) = refs[:12], refs[12:14]
    chol, amp, window, spread, straight, turned, occ, *sems = refs[14:]
    x, oj, vert, core, flip, first = place_of()
    where = []
    for tile in range(12):
        for a in range(3):
            for at in (2 * tile, 2 * tile + 1):
                where.append((at // 3, a, at % 3))
    slots = [(a, b) for a in range(3) for b in range(3)]
    sym = begin(
        occ_ref, amp_ref, pieces, chol, amp, occ, sems, flip, first, x, oj, slots, turned
    )
    own_ref[...] = jnp.zeros_like(own_ref)
    mirror_ref[...] = jnp.zeros_like(mirror_ref)

    def one_irrep(ga, carry):
        amp_copy(amp_ref, amp, sems[1], flip, ga).wait()
        spread_out(amp[ga], spread)
        left = chol[ga].reshape(3 * VB, PB)
        for tile in range(12):
            two = [chol[at // 3, at % 3] for at in (2 * tile, 2 * tile + 1)]
            block = lax.dot_general(
                left, jnp.concatenate(two, 0), NT, preferred_element_type=jnp.float32
            )
            for a in range(3):
                store_block(window, (tile * 3 + a) * 2 * LO, block, a * VB)
        full = []
        for start, stop in ((0, 32), (32, 72)):
            rows = window[start * LO : stop * LO]
            part = lax.dot_general(rows, spread[...], NT, preferred_element_type=jnp.float32)
            full.append(part.reshape(stop - start, LO, COLS))
        collect(jnp.concatenate(full, 0), sym, ga, where, straight, turned)
        return carry

    lax.fori_loop(0, IRREPS, one_irrep, 0)
    finish(slots, straight, turned, own_ref, mirror_ref, x, core, vert)


def late_kernel(occ_ref, amp_ref, own_in, mirror_in, *refs):
    pieces, (own_ref, mirror_ref) = refs[:13], refs[13:15]
    chol, amp, window, spread, straight, turned, occ, *sems = refs[15:]
    x, oj, vert, core, flip, first = place_of()
    where = []
    for tile in range(4):
        for a in range(4):
            where += [(2 * tile, a, 3), (2 * tile + 1, a, 3)]
    for at in range(24):
        where.append((at // 3, 3, at % 3))
    slots = [(a, 3) for a in range(4)] + [(3, b) for b in range(3)]
    sym = begin(
        occ_ref, amp_ref, pieces, chol, amp, occ, sems, flip, first, x, oj, slots, turned
    )
    own_ref[...] = own_in[...]
    mirror_ref[...] = mirror_in[...]

    def two_irreps(step, carry):
        last = chol[pl.ds(2 * step, 2), 3].reshape(2 * VB, PB)
        for tile in range(12):
            two = [chol[at // 3, at % 3] for at in (2 * tile, 2 * tile + 1)]
            block = lax.dot_general(
                last, jnp.concatenate(two, 0), NT, preferred_element_type=jnp.float32
            )
            for u in range(2):
                store_block(window, (32 + 24 * u + 2 * tile) * LO, block, u * VB)

        def one_irrep(u, carry):
            ga = 2 * step + u
            amp_copy(amp_ref, amp, sems[1], flip, ga).wait()
            spread_out(amp[ga], spread)
            left = chol[ga].reshape(WB * VB, PB)
            for tile in range(4):
                two = [chol[2 * tile, 3], chol[2 * tile + 1, 3]]
                block = lax.dot_general(
                    left, jnp.concatenate(two, 0), NT, preferred_element_type=jnp.float32
                )
                for a in range(WB):
                    store_block(window, (tile * WB + a) * 2 * LO, block, a * VB)
            lower = window[pl.ds(pl.multiple_of((32 + 24 * u) * LO, 2 * LO), 24 * LO)]
            for rows, start, stop in ((window[: 32 * LO], 0, 32), (lower, 32, 56)):
                part = lax.dot_general(rows, spread[...], NT, preferred_element_type=jnp.float32)
                part = part.reshape(stop - start, LO, COLS)
                collect(part, sym, ga, where[start:stop], straight, turned)
            return carry

        return lax.fori_loop(0, 2, one_irrep, carry)

    lax.fori_loop(0, IRREPS // 2, two_irreps, 0)
    finish(slots, straight, turned, own_ref, mirror_ref, x, core, vert)


def ladder(kernel, slots, window, before, pieces):
    anywhere = pl.BlockSpec(memory_space=pl.ANY)
    whole = pl.BlockSpec(memory_space=pltpu.VMEM)
    occ, amp, *earlier = before
    return pl.pallas_call(
        kernel,
        out_shape=[
            jax.ShapeDtypeStruct((IRREPS, WB, VB), jnp.float32),
            jax.ShapeDtypeStruct((IRREPS, WB, VB), jnp.float32),
        ],
        in_specs=[anywhere] * 2 + [whole] * len(earlier) + [anywhere] * len(pieces),
        out_specs=[whole] * 2,
        scratch_shapes=[
            pltpu.VMEM((IRREPS, slots, VB, PB), jnp.bfloat16),
            pltpu.VMEM((IRREPS, PAIRS, VB, VB), jnp.bfloat16),
            pltpu.VMEM(window + (HI * VB,), jnp.bfloat16),
            pltpu.VMEM((COLS, HI * VB), jnp.bfloat16),
            pltpu.VMEM((IRREPS, WB * WB, LO, COLS), jnp.float32),
            pltpu.VMEM((IRREPS, WB * WB, LO, COLS), jnp.float32),
            pltpu.SMEM((PAIRS,), jnp.int32),
            pltpu.SemaphoreType.DMA((16,)),
            pltpu.SemaphoreType.DMA((8,)),
            pltpu.SemaphoreType.DMA,
        ],
        compiler_params=pltpu.CompilerParams(vmem_limit_bytes=50 * 2**20),
        cost_estimate=pl.CostEstimate(
            flops=8 * 10**9, bytes_accessed=12 * 10**6, transcendentals=0
        ),
    )(*before, *pieces)


def local(amplitudes, chol, occ_irrep):
    x = lax.axis_index("oi")
    core = lax.rem(lax.axis_index("oj"), 2)

    def permute(value, pairs):
        return lax.ppermute(value, AXES, pairs)

    mine = lax.dynamic_index_in_dim(chol[0], x, 1, False).T
    pair = jnp.stack([mine, permute(mine, moved_pairs(next_row))])
    near = [permute(pair, fetch_pairs(row)) for row in (0, 2)]
    near[1], labels = lax.optimization_barrier((near[1], jnp.bitwise_and(occ_irrep, IRREPS - 1)))
    above = [permute(half, moved_pairs(lower)) for half in near]
    below = [permute(half, moved_pairs(upper)) for half in near]
    swap = moved_pairs(other_core)
    beside = [permute(jnp.stack([above[far], below[far]]), swap) for far in range(2)]
    pieces = near + [permute(half, swap) for half in near]
    pieces += above + [beside[0][0], beside[1][0]] + below + [beside[0][1], beside[1][1]]
    beyond = jnp.where(core == 0, jnp.stack(pieces[4:8]), jnp.stack(pieces[8:12]))
    beyond = permute(beyond, moved_pairs(apart))
    occ_rows, occ_cols = amplitudes.shape[0], amplitudes.shape[1]
    amp = amplitudes.reshape(PAIRS, IRREPS, VB, VB)
    before = (labels, amp)
    mine, other = ladder(early_kernel, 3, (72 * LO,), before, pieces)
    before += (mine, other)
    pieces += [beyond]
    mine, other = ladder(late_kernel, 4, (80 * LO,), before, pieces)
    every = jnp.concatenate([mine, other], axis=1)
    every = jnp.sum(lax.all_to_all(every, "vert", 0, 0), axis=0)
    other = every[WB:]
    given = permute(other, moved_pairs(other_core))
    side = jnp.arange(VB, dtype=jnp.int32)[None, :] // 16 % 2
    given = jnp.where(side == 0, jnp.roll(given, -16, 1), jnp.roll(given, 16, 1))
    other = jnp.where(side == core, other, given)
    total = every[:WB] + permute(other, moved_pairs(mirrored))
    total = total.reshape(WB, WB, occ_rows, occ_cols)
    return jnp.transpose(total, (2, 3, 0, 1))[:, :, None]


def solution(mesh):
    return jax.shard_map(
        local,
        mesh=mesh,
        in_specs=(P("oi", "oj", None, None, None), P(("oj", "vert"), None, None, None), P()),
        out_specs=P("oi", "oj", "vert", None, None),
        check_vma=False,
    )
```

```python
import jax
import jax.numpy as jnp
from jax import lax
from jax.experimental import pallas as pl
from jax.experimental.pallas import tpu as pltpu
from jax.sharding import PartitionSpec as P

IRREPS = 8
VB = 128
PB = 256
WB = 4
LO = 8
HI = VB // LO
PAIRS = 32
HOPS = (0, 1, 3, 2)
COLS = PAIRS * LO
AXES = ("oi", "oj", "vert")
CHIPS = [
    (x, zh, core, zl, y)
    for x in range(4)
    for zh in range(4)
    for core in range(2)
    for zl in range(2)
    for y in range(4)
]
NT = (((1,), (1,)), ((), ()))


def flat_index(x, zh, core, zl, y):
    return x * 64 + (zh * 2 + core) * 8 + zl * 4 + y


def fetch_pairs(row):
    pairs = []
    for x, zh, core, zl, y in CHIPS:
        source = (x, (zh + y + 2 * zl) % 4, zl, core, y ^ row)
        pairs.append((flat_index(*source), flat_index(x, zh, core, zl, y)))
    return pairs


def moved_pairs(move):
    return [(flat_index(*d), flat_index(*move(*d))) for d in CHIPS]


def next_row(x, zh, core, zl, y):
    return (x, zh, core, zl, y ^ 1)


def lower(x, zh, core, zl, y):
    return ((x + 3) % 4, zh, core, zl, y)


def upper(x, zh, core, zl, y):
    return ((x + 1) % 4, zh, core, zl, y)


def apart(x, zh, core, zl, y):
    return ((x + (1 if core else 3)) % 4, zh, core, zl, y)


def other_core(x, zh, core, zl, y):
    return (x, zh, 1 - core, zl, y)


def mirrored(x, zh, core, zl, y):
    return (zh, x, core, zl, y)


def exact_pick(values, chosen):
    top = values.astype(jnp.bfloat16)
    rest = values - top.astype(jnp.float32)
    middle = rest.astype(jnp.bfloat16)
    low = (rest - middle.astype(jnp.float32)).astype(jnp.bfloat16)
    rows = values.shape[0]
    parts = jnp.dot(
        jnp.concatenate([top, middle, low], 0), chosen, preferred_element_type=jnp.float32
    )
    return parts[:rows] + (parts[rows : 2 * rows] + parts[2 * rows :])


def place_of():
    x, oj, vert = lax.axis_index("oi"), lax.axis_index("oj"), lax.axis_index("vert")
    zh, core, zl, y = oj // 2, lax.rem(oj, 2), vert // 4, lax.rem(vert, 4)
    block = lax.rem(zh + y + 2 * zl, 4) * 2 + zl
    return x, oj, vert, core, jnp.bitwise_xor(block, vert), jnp.bitwise_xor(core, zl)


def load_pieces(pieces, chol, sems, first):
    pieces = list(pieces[:12]) + [beyond.at[at] for beyond in pieces[12:] for at in range(4)]
    copies = []
    for at, piece in enumerate(pieces):
        half = first if at // 2 % 2 == 0 else 1 - first
        target = chol.at[pl.ds(half * 4 + 2 * (at % 2), 2), at // 4]
        copies.append(pltpu.make_async_copy(piece, target, sems.at[at]))
    return copies


def pair_labels(occ, x, oj):
    pair = lax.broadcasted_iota(jnp.int32, (1, COLS), 1) // LO
    sym = jnp.zeros((1, COLS), jnp.int32)
    for row in range(8):
        for col in range(4):
            label = jnp.bitwise_xor(occ[x * 8 + row], occ[oj * 4 + col])
            sym = jnp.where(pair == row * 4 + col, label, sym)
    lo_row = lax.broadcasted_iota(jnp.int32, (LO, COLS), 0)
    lo_col = lax.broadcasted_iota(jnp.int32, (LO, COLS), 1) % LO
    return jnp.where(lo_row == lo_col, sym, -1)


def store_block(window, base, block, row):
    for hi in range(HI):
        at = row + hi * LO
        window[base : base + 2 * LO, hi * VB : (hi + 1) * VB] = jnp.concatenate(
            [block[at : at + LO, :VB], block[at : at + LO, VB:]], 0
        ).astype(jnp.bfloat16)


def spread_out(amp, spread):
    wide = amp.astype(jnp.float32).reshape(PAIRS, HI, LO, VB)
    for hi in range(HI):
        spread[:, hi * VB : (hi + 1) * VB] = wide[:, hi].reshape(COLS, VB).astype(jnp.bfloat16)


def collect(full, sym, ga, where, straight, turned):
    totals = {}
    for at, (gb, a, b) in enumerate(where):
        wanted = sym == jnp.bitwise_xor(ga, gb)
        slot = WB * a + b
        totals[slot] = jnp.where(wanted, full[at], totals.get(slot, 0.0))
        turned[gb, slot] = jnp.where(wanted, full[at], turned[gb, slot])
    for slot, total in totals.items():
        straight[ga, slot] = total


def finish(slots, straight, turned, own_ref, mirror_ref, x, core, vert):
    count = len(slots)
    actual = [lax.rem(x + hop, WB) for hop in HOPS]
    source = lax.broadcasted_iota(jnp.int32, (COLS, VB), 0) // LO
    lane = lax.broadcasted_iota(jnp.int32, (COLS, VB), 1) % PAIRS
    group = lax.broadcasted_iota(jnp.int32, (IRREPS, VB), 1) // PAIRS

    def summed(values):
        rows = [jnp.sum(values[:, WB * a + b], axis=1) for a, b in slots]
        return jnp.concatenate(rows, 0)

    def split(values, chosen, by_first):
        picked = exact_pick(values, chosen)
        lines = {}
        for at, (a, b) in enumerate(slots):
            line, wide = (a, b) if by_first else (b, a)
            part = jnp.where(group == actual[wide], picked[at * IRREPS : (at + 1) * IRREPS], 0.0)
            lines[line] = lines.get(line, 0.0) + part
        return lines

    own = split(summed(straight), (source == lane).astype(jnp.bfloat16), True)
    for line, value in own.items():
        for ga in range(IRREPS):
            there = (jnp.bitwise_xor(vert, ga), pl.ds(actual[line], 1))
            own_ref[there] = own_ref[there] + value[ga : ga + 1]
    every = summed(turned)
    target = core * 16 + (source % 4) * 4 + (source // 4) % 4
    for k in range(2):
        here = (source // 16) == jnp.bitwise_xor(core, k)
        other = split(every, ((lane == target) & here).astype(jnp.bfloat16), False)
        for line, value in other.items():
            for ga in range(IRREPS):
                there = (k, jnp.bitwise_xor(vert, ga), pl.ds(actual[line], 1))
                mirror_ref[there] = mirror_ref[there] + value[ga : ga + 1]


def amp_copy(amp_ref, amp, sems, flip, ga):
    return pltpu.make_async_copy(
        amp_ref.at[:, jnp.bitwise_xor(ga, flip)], amp.at[ga], sems.at[ga]
    )


def begin(occ_ref, amp_ref, pieces, chol, amp, occ, sems, flip, first, x, oj, slots, turned):
    chol_sem, amp_sem, occ_sem = sems
    occ_copy = pltpu.make_async_copy(occ_ref, occ, occ_sem)
    occ_copy.start()
    amp_copy(amp_ref, amp, amp_sem, flip, 0).start()
    copies = load_pieces(pieces, chol, chol_sem, first)
    for copy in copies:
        copy.start()
    occ_copy.wait()
    sym = pair_labels(occ, x, oj)
    for a, b in slots:
        turned[:, WB * a + b] = jnp.zeros((IRREPS, LO, COLS), jnp.float32)
    for copy in copies:
        copy.wait()
    for ga in range(1, IRREPS):
        amp_copy(amp_ref, amp, amp_sem, flip, ga).start()
    return sym


def early_kernel(occ_ref, amp_ref, *refs):
    pieces, (own_ref, mirror_ref) = refs[:12], refs[12:14]
    chol, amp, window, spread, straight, turned, occ, *sems = refs[14:]
    x, oj, vert, core, flip, first = place_of()
    where = []
    for tile in range(12):
        for a in range(3):
            for at in (2 * tile, 2 * tile + 1):
                where.append((at // 3, a, at % 3))
    slots = [(a, b) for a in range(3) for b in range(3)]
    sym = begin(
        occ_ref, amp_ref, pieces, chol, amp, occ, sems, flip, first, x, oj, slots, turned
    )
    own_ref[...] = jnp.zeros_like(own_ref)
    mirror_ref[...] = jnp.zeros_like(mirror_ref)

    def one_irrep(ga, carry):
        amp_copy(amp_ref, amp, sems[1], flip, ga).wait()
        spread_out(amp[ga], spread)
        left = chol[ga].reshape(3 * VB, PB)
        for tile in range(12):
            two = [chol[at // 3, at % 3] for at in (2 * tile, 2 * tile + 1)]
            block = lax.dot_general(
                left, jnp.concatenate(two, 0), NT, preferred_element_type=jnp.float32
            )
            for a in range(3):
                store_block(window, (tile * 3 + a) * 2 * LO, block, a * VB)
        full = []
        for start, stop in ((0, 32), (32, 72)):
            rows = window[start * LO : stop * LO]
            part = lax.dot_general(rows, spread[...], NT, preferred_element_type=jnp.float32)
            full.append(part.reshape(stop - start, LO, COLS))
        collect(jnp.concatenate(full, 0), sym, ga, where, straight, turned)
        return carry

    lax.fori_loop(0, IRREPS, one_irrep, 0)
    finish(slots, straight, turned, own_ref, mirror_ref, x, core, vert)


def late_kernel(occ_ref, amp_ref, own_in, mirror_in, *refs):
    pieces, (own_ref, mirror_ref) = refs[:13], refs[13:15]
    chol, amp, window, spread, straight, turned, occ, *sems = refs[15:]
    x, oj, vert, core, flip, first = place_of()
    where = []
    for tile in range(4):
        for a in range(4):
            where += [(2 * tile, a, 3), (2 * tile + 1, a, 3)]
    for at in range(24):
        where.append((at // 3, 3, at % 3))
    slots = [(a, 3) for a in range(4)] + [(3, b) for b in range(3)]
    sym = begin(
        occ_ref, amp_ref, pieces, chol, amp, occ, sems, flip, first, x, oj, slots, turned
    )
    own_ref[...] = own_in[...]
    mirror_ref[...] = mirror_in[...]

    def two_irreps(step, carry):
        last = chol[pl.ds(2 * step, 2), 3].reshape(2 * VB, PB)
        for tile in range(12):
            two = [chol[at // 3, at % 3] for at in (2 * tile, 2 * tile + 1)]
            block = lax.dot_general(
                last, jnp.concatenate(two, 0), NT, preferred_element_type=jnp.float32
            )
            for u in range(2):
                store_block(window, (32 + 24 * u + 2 * tile) * LO, block, u * VB)

        def one_irrep(u, carry):
            ga = 2 * step + u
            amp_copy(amp_ref, amp, sems[1], flip, ga).wait()
            spread_out(amp[ga], spread)
            left = chol[ga].reshape(WB * VB, PB)
            for tile in range(4):
                two = [chol[2 * tile, 3], chol[2 * tile + 1, 3]]
                block = lax.dot_general(
                    left, jnp.concatenate(two, 0), NT, preferred_element_type=jnp.float32
                )
                for a in range(WB):
                    store_block(window, (tile * WB + a) * 2 * LO, block, a * VB)
            lower = window[pl.ds(pl.multiple_of((32 + 24 * u) * LO, 2 * LO), 24 * LO)]
            for rows, start, stop in ((window[: 32 * LO], 0, 32), (lower, 32, 56)):
                part = lax.dot_general(rows, spread[...], NT, preferred_element_type=jnp.float32)
                part = part.reshape(stop - start, LO, COLS)
                collect(part, sym, ga, where[start:stop], straight, turned)
            return carry

        return lax.fori_loop(0, 2, one_irrep, carry)

    lax.fori_loop(0, IRREPS // 2, two_irreps, 0)
    finish(slots, straight, turned, own_ref, mirror_ref, x, core, vert)


def ladder(kernel, slots, window, before, pieces):
    anywhere = pl.BlockSpec(memory_space=pl.ANY)
    whole = pl.BlockSpec(memory_space=pltpu.VMEM)
    occ, amp, *earlier = before
    return pl.pallas_call(
        kernel,
        out_shape=[
            jax.ShapeDtypeStruct((IRREPS, WB, VB), jnp.float32),
            jax.ShapeDtypeStruct((2, IRREPS, WB, VB), jnp.float32),
        ],
        in_specs=[anywhere] * 2 + [whole] * len(earlier) + [anywhere] * len(pieces),
        out_specs=[whole] * 2,
        scratch_shapes=[
            pltpu.VMEM((IRREPS, slots, VB, PB), jnp.bfloat16),
            pltpu.VMEM((IRREPS, PAIRS, VB, VB), jnp.bfloat16),
            pltpu.VMEM(window + (HI * VB,), jnp.bfloat16),
            pltpu.VMEM((COLS, HI * VB), jnp.bfloat16),
            pltpu.VMEM((IRREPS, WB * WB, LO, COLS), jnp.float32),
            pltpu.VMEM((IRREPS, WB * WB, LO, COLS), jnp.float32),
            pltpu.SMEM((PAIRS,), jnp.int32),
            pltpu.SemaphoreType.DMA((16,)),
            pltpu.SemaphoreType.DMA((8,)),
            pltpu.SemaphoreType.DMA,
        ],
        compiler_params=pltpu.CompilerParams(vmem_limit_bytes=50 * 2**20),
        cost_estimate=pl.CostEstimate(
            flops=8 * 10**9, bytes_accessed=12 * 10**6, transcendentals=0
        ),
    )(*before, *pieces)


def local(amplitudes, chol, occ_irrep):
    x = lax.axis_index("oi")
    core = lax.rem(lax.axis_index("oj"), 2)

    def permute(value, pairs):
        return lax.ppermute(value, AXES, pairs)

    mine = lax.dynamic_index_in_dim(chol[0], x, 1, False).T
    pair = jnp.stack([mine, permute(mine, moved_pairs(next_row))])
    near = [permute(pair, fetch_pairs(row)) for row in (0, 2)]
    above = [permute(half, moved_pairs(lower)) for half in near]
    below = [permute(half, moved_pairs(upper)) for half in near]
    labels = jnp.bitwise_and(occ_irrep, IRREPS - 1)
    above[1], labels = lax.optimization_barrier((above[1], labels))
    swap = moved_pairs(other_core)
    beside = [permute(jnp.stack([above[far], below[far]]), swap) for far in range(2)]
    pieces = near + [permute(half, swap) for half in near]
    pieces += above + [beside[0][0], beside[1][0]] + below + [beside[0][1], beside[1][1]]
    beyond = jnp.where(core == 0, jnp.stack(pieces[4:8]), jnp.stack(pieces[8:12]))
    beyond = permute(beyond, moved_pairs(apart))
    occ_rows, occ_cols = amplitudes.shape[0], amplitudes.shape[1]
    amp = amplitudes.reshape(PAIRS, IRREPS, VB, VB)
    before = (labels, amp)
    mine, other = ladder(early_kernel, 3, (72 * LO,), before, pieces)
    before += (mine, other)
    pieces += [beyond]
    mine, other = ladder(late_kernel, 4, (80 * LO,), before, pieces)
    every = jnp.concatenate([mine, other[0], other[1]], axis=1)
    every = jnp.sum(lax.all_to_all(every, "vert", 0, 0), axis=0)
    other = every[WB : 2 * WB] + permute(every[2 * WB :], moved_pairs(other_core))
    total = every[:WB] + permute(other, moved_pairs(mirrored))
    total = total.reshape(WB, WB, occ_rows, occ_cols)
    return jnp.transpose(total, (2, 3, 0, 1))[:, :, None]


def solution(mesh):
    return jax.shard_map(
        local,
        mesh=mesh,
        in_specs=(P("oi", "oj", None, None, None), P(("oj", "vert"), None, None, None), P()),
        out_specs=P("oi", "oj", "vert", None, None),
        check_vma=False,
    )
```
